32 devices in a mesh: dp: 4 (over y, x), ctx: 8 (over z, core).
Axes of the slice: x: 2, y: 2, z: 4, core: 2. Of those that a mesh axis runs over, the one named last changes fastest.
Arguments:
- hidden_in: bfloat16 [4, 3072, 576], P('dp', 'ctx'), may hold values from -6 to 6
- segment_ids: int32 [4, 3072], P('dp', 'ctx'), may hold values from 0 to 3, as said below
- w_query: bfloat16 [576, 576], replicated, may hold values from -0.625 to 0.625
- w_key: bfloat16 [576, 192], replicated, may hold values from -0.25 to 0.25
- w_value: bfloat16 [576, 192], replicated, may hold values from -0.25 to 0.25
- w_out: bfloat16 [576, 576], replicated, may hold values from -0.5 to 0.5
- w_gate: bfloat16 [576, 1536], replicated, may hold values from -0.25 to 0.25
- w_up: bfloat16 [576, 1536], replicated, may hold values from -0.25 to 0.25
- w_down: bfloat16 [1536, 576], replicated, may hold values from -0.15625 to 0.15625
- gain_attn: float32 [576], replicated, may hold values from 0.1 to 1.9
- gain_ffn: float32 [576], replicated, may hold values from 0.1 to 1.9
- out_grad: bfloat16 [4, 3072, 576], P('dp', 'ctx'), may hold values from -6 to 6
Outputs:
- layer_out: bfloat16 [4, 3072, 576], P('dp', 'ctx')
- input_grad: bfloat16 [4, 3072, 576], P('dp', 'ctx')
- grad_query: float32 [576, 576], replicated
- grad_key: float32 [576, 192], replicated
- grad_value: float32 [576, 192], replicated
- grad_out: float32 [576, 576], replicated
- grad_gate: float32 [576, 1536], replicated
- grad_up: float32 [576, 1536], replicated
- grad_down: float32 [1536, 576], replicated
- grad_gain_attn: float32 [576], replicated
- grad_gain_ffn: float32 [576], replicated
The draws below stay inside these ranges and needn't reach their ends.
Inputs may be any that keep to these rules, and one draw needn't show every extreme that they name: `segment_ids`: ids never fall along a sequence and start at 0; in every sequence one document starts within the first 384 positions and ends within the last 384.
All inputs are finite; a program needn't handle non-finite values.
Results may differ from the reference program's by a relative error of at most 0.02.
Values may be sent and summed in bfloat16 or wider, within the bound.
A program may use at most 128 MiB of HBM per device.

```python
import math
import jax
import jax.numpy as jnp
from jax import lax

D = 576
HEADS = 9
KV_HEADS = 3
HEAD_DIM = 64
FF = 1536
TOK_DEV = 384
SEQS = 4
SEQ_LEN = 3072


def draw_segment_ids(key, part):
    key = jax.random.fold_in(key, 7)
    first_key, second_key, third_key = jax.random.split(key, 3)
    begin_at = jax.random.randint(first_key, (SEQS, 1), 1, TOK_DEV)
    early_at = 1 + jax.random.randint(second_key, (SEQS, 1), 0, TOK_DEV) % begin_at
    finish_at = jax.random.randint(third_key, (SEQS, 1), SEQ_LEN - TOK_DEV + 1, SEQ_LEN)
    places = jnp.arange(SEQ_LEN, dtype=jnp.int32)[None, :]
    return (places >= early_at).astype(jnp.int32) + (places >= begin_at).astype(jnp.int32) + (places >= finish_at).astype(jnp.int32)


def level_of(key, shape, pieces, smallest, high):
    def one(dim, shards_of):
        heights = jax.random.uniform(jax.random.fold_in(jax.random.fold_in(key, 6), dim), (shards_of,), jnp.float32, smallest / len(pieces), high / len(pieces))
        return jnp.repeat(jnp.exp(heights), shape[dim] // shards_of).reshape((-1,) + (1,) * (len(shape) - dim - 1))

    loudness = one(*pieces[0])
    for cut in pieces[1:]:
        loudness = loudness * one(*cut)
    return loudness


def normal_values(key, dims, scale, reach, pieces=(), kind=jnp.bfloat16):
    factor_of = level_of(key, dims, pieces, -0.22, 0.18) if pieces else 1.0
    entries = jax.random.normal(key, dims, jnp.float32) * scale * factor_of
    return jnp.minimum(jnp.maximum(entries, -reach), reach).astype(kind)


def setup_inputs(seed: int = 0) -> dict:
    seeds = jax.random.split(jax.random.key(seed), 13)
    return {
        "hidden_in": normal_values(seeds[0], (SEQS, SEQ_LEN, D), 1.0, 6.0, ((0, 4), (1, 8))),
        "segment_ids": draw_segment_ids(jax.random.fold_in(seeds[12], 71), 0),
        "w_query": normal_values(seeds[2], (D, D), (D // 6) ** -0.5, 0.625),
        "w_key": normal_values(seeds[3], (D, KV_HEADS * HEAD_DIM), D ** -0.5, 0.25),
        "w_value": normal_values(seeds[4], (D, KV_HEADS * HEAD_DIM), D ** -0.5, 0.25),
        "w_out": normal_values(seeds[5], (D, D), (D // 4) ** -0.5, 0.5),
        "w_gate": normal_values(seeds[6], (D, FF), D ** -0.5, 0.25),
        "w_up": normal_values(seeds[7], (D, FF), D ** -0.5, 0.25),
        "w_down": normal_values(seeds[8], (FF, D), FF ** -0.5, 0.15625),
        "gain_attn": jnp.clip(1.0 + 0.18 * jax.random.normal(seeds[9], (D,), jnp.float32), 0.1, 1.9),
        "gain_ffn": jnp.clip(1.0 + 0.18 * jax.random.normal(seeds[10], (D,), jnp.float32), 0.1, 1.9),
        "out_grad": normal_values(seeds[11], (SEQS, SEQ_LEN, D), 1.0, 6.0, ((0, 4), (1, 8))),
    }


@jax.custom_vjp
def low(v):
    return lax.optimization_barrier(v.astype(jnp.bfloat16)).astype(jnp.float32)

@jax.custom_vjp
def low_back(v):
    return v

def low_keep(v):
    return (low(v), None)

def low_pass(kept, grad):
    return (grad,)

def back_keep(v):
    return (v, None)

def back_low(kept, grad):
    return (low(grad),)
low.defvjp(low_keep, low_pass)
low_back.defvjp(back_keep, back_low)
NORM_EPS = 1e-05
ROPE_BASE = 10000.0
MASKED = -1e+30
HIGH = lax.Precision.HIGHEST

def product(left_side, right_side):
    return jnp.dot(left_side, right_side, precision=HIGH)

def rms_norm(values, gain_vector):
    return values * lax.rsqrt(lax.optimization_barrier(jnp.mean(values * values, axis=-1, keepdims=True)) + NORM_EPS) * gain_vector

def rotate(values, positions):
    head_size = values.shape[-1]
    half_size = head_size // 2
    inverse = ROPE_BASE ** (-jnp.arange(half_size, dtype=jnp.float32) * 2.0 / head_size)
    phase_angle = positions.astype(jnp.float32)[:, None] * inverse[None, :]
    cosine = jnp.cos(phase_angle)[:, None, :]
    sine_table = jnp.sin(phase_angle)[:, None, :]
    first_half = values[..., :half_size]
    second_half = values[..., half_size:]
    return jnp.concatenate([first_half * cosine - second_half * sine_table, second_half * cosine + first_half * sine_table], axis=-1)

def attend(query_rows, key_rows, value_rows, seq_ids):
    seq_rows = query_rows.shape[0]
    block_rows = math.gcd(seq_rows, 512)
    key_index = jnp.arange(seq_rows, dtype=jnp.int32)
    score_scale = 1.0 / math.sqrt(HEAD_DIM)

    def query_block(block_index):
        first_row = (block_index * block_rows).astype(jnp.int32)
        block_query = lax.dynamic_slice_in_dim(query_rows, first_row, block_rows, 0)
        block_ids = lax.dynamic_slice_in_dim(seq_ids, first_row, block_rows, 0)
        row_index = first_row + jnp.arange(block_rows, dtype=jnp.int32)
        allowed = (block_ids[:, None] == seq_ids[None, :]) & (key_index[None, :] <= row_index[:, None])
        scores = low_back(jnp.einsum('qhgd,khd->hgqk', block_query, key_rows, precision=HIGH) * score_scale)
        scores = jnp.where(allowed, scores, MASKED)
        row_max = lax.optimization_barrier(jnp.max(scores, axis=-1, keepdims=True))
        weights = jnp.exp(scores - row_max)
        prob_rows = low(weights / lax.optimization_barrier(jnp.sum(weights, axis=-1, keepdims=True)))
        return jnp.einsum('hgqk,khd->qhgd', prob_rows, value_rows, precision=HIGH)
    blocks = lax.map(jax.checkpoint(query_block), jnp.arange(seq_rows // block_rows, dtype=jnp.int32))
    return blocks.reshape(seq_rows, HEADS * HEAD_DIM)

def decoder_layer(inputs, seq_ids, w_query, w_key, w_value, w_out, w_gate, w_up, w_down, gain_attn, gain_ffn):
    seq_rows = inputs.shape[0]
    index_rows = jnp.arange(seq_rows, dtype=jnp.int32)
    positions = index_rows - jnp.searchsorted(seq_ids, seq_ids, side='left').astype(jnp.int32)
    normed = low(rms_norm(inputs, gain_attn))
    query_rows = low_back(product(normed, w_query)).reshape(seq_rows, HEADS, HEAD_DIM)
    query_rows = low(rotate(query_rows, positions)).reshape(seq_rows, KV_HEADS, HEADS // KV_HEADS, HEAD_DIM)
    key_rows = low_back(product(normed, w_key)).reshape(seq_rows, KV_HEADS, HEAD_DIM)
    key_rows = low(rotate(key_rows, positions))
    value_rows = low(low_back(product(normed, w_value))).reshape(seq_rows, KV_HEADS, HEAD_DIM)
    attn_mixed = low(low_back(attend(query_rows, key_rows, value_rows, seq_ids)))
    residual = inputs + low_back(product(attn_mixed, w_out))
    normed_ffn = low(rms_norm(residual, gain_ffn))
    gate_rows = low_back(product(normed_ffn, w_gate))
    up_rows = low_back(product(normed_ffn, w_up))
    hidden = low(jax.nn.silu(gate_rows) * up_rows)
    return residual + low_back(product(hidden, w_down))

def reference(hidden_in, segment_ids, w_query, w_key, w_value, w_out, w_gate, w_up, w_down, gain_attn, gain_ffn, out_grad):
    weight_list = (w_query.astype(jnp.float32), w_key.astype(jnp.float32), w_value.astype(jnp.float32), w_out.astype(jnp.float32), w_gate.astype(jnp.float32), w_up.astype(jnp.float32), w_down.astype(jnp.float32), gain_attn.astype(jnp.float32), gain_ffn.astype(jnp.float32))

    def per_sequence(totals, item_in):
        inputs, seq_ids, cotangent = item_in

        def forward(inputs_f, *weights_f):
            return decoder_layer(inputs_f, seq_ids, *weights_f)
        result, pullback = jax.vjp(forward, inputs.astype(jnp.float32), *weight_list)
        gradient_list = pullback(cotangent.astype(jnp.float32))
        totals = tuple((total_grad + new_grad for total_grad, new_grad in zip(totals, gradient_list[1:])))
        return (totals, (result.astype(jnp.bfloat16), gradient_list[0].astype(jnp.bfloat16)))
    start_totals = tuple((jnp.zeros(weight.shape, jnp.float32) for weight in weight_list))
    totals, (layer_out, input_grad) = lax.scan(per_sequence, start_totals, (hidden_in, segment_ids, out_grad))
    return (layer_out, input_grad, totals[0], totals[1], totals[2], totals[3], totals[4], totals[5], totals[6], totals[7], totals[8])
```

```python
import functools
import math

import jax
import jax.numpy as jnp
import numpy as np
from jax import lax
from jax.experimental import pallas as pl
from jax.experimental.pallas import tpu as pltpu
from jax.sharding import PartitionSpec as P

HEADS = 9
KV_HEADS = 3
HEAD_DIM = 64
GROUPS = HEADS // KV_HEADS

NORM_EPS = 1e-05
ROPE_BASE = 10000.0
MASKED = -1e30
LOG2E = 1.4426950408889634
LN2 = 0.6931471805599453
MESH = pl.DeviceIdType.MESH
OUT_ROWS = 640
QUERY_COLUMNS = 256
ID_ROWS = 16
CHUNK = 256
FF_CHUNK = 512
BACK_CHUNK = 384


def matmul(left_side, right_side):
    return jnp.dot(left_side, right_side, preferred_element_type=jnp.float32)


def times_transposed(left_side, right_side):
    return lax.dot_general(
        left_side, right_side, (((1,), (1,)), ((), ())), preferred_element_type=jnp.float32
    )


def transposed_times(left_side, right_side):
    return lax.dot_general(
        left_side, right_side, (((0,), (0,)), ((), ())), preferred_element_type=jnp.float32
    )


def bit_of(place, bit):
    return lax.rem(lax.div(place, bit), 2)


def flipped(axis, bit):
    place = lax.axis_index(axis)
    return {axis: place + (1 - 2 * bit_of(place, bit)) * bit}


def plane_order(dp_count):
    bits = [1 << i for i in range(dp_count.bit_length() - 1)]
    return [("ctx", 1, 1)] + [("dp", bit, bits[(i + 1) % len(bits)]) for i, bit in enumerate(bits)]


def mirrored(size):
    place = lax.axis_index("ctx")
    core, level = lax.rem(place, 2), lax.div(place, 2)
    group = lax.div(level, size) * size
    return {"ctx": 2 * (2 * group + size - 1 - level) + core}


def is_inner(level):
    return lax.rem(level, 2) != lax.rem(lax.div(level, 2), 2)


HALVINGS = 3


def halved_shapes(rows, columns, cuts):
    shapes = []
    for cut in cuts:
        rows, columns = (rows // 2, columns) if cut == "r" else (rows, columns // 2)
        shapes.append((rows, columns))
    return shapes


def landing_shapes(rows, columns, cuts, plane, level_bits):
    shapes = halved_shapes(rows, columns, cuts)
    return shapes + [shapes[-1]] * (plane - len(cuts) + level_bits + 1)


class Summed:
    def __init__(self, order, level_bits, cuts, source, corner, shape, landed, total, send, recv):
        self.order, self.level_bits, self.cuts = order, level_bits, cuts
        self.landed, self.total = landed, total
        self.source, self.corner, self.shape = source, corner, shape
        self.send, self.recv = send, recv
        self.plane = len(order)
        self.count = self.plane + level_bits + 1
        self.final = landed[-1]

    def cut_at(self, corner, shape, cut, pick):
        rows, columns = shape
        row, column = corner
        if cut == "r":
            rows //= 2
            row = row + pick * rows
        else:
            columns //= 2
            column = column + pick * columns
        return (row, column), (rows, columns)

    @staticmethod
    def view(ref, corner, shape):
        row, column = corner
        if not isinstance(row, int):
            row = pl.multiple_of(row, 16)
        if not isinstance(column, int):
            column = pl.multiple_of(column, 128)
        return ref.at[pl.ds(row, shape[0]), pl.ds(column, shape[1])]

    def current(self, stage):
        if stage == 0:
            return self.source, self.corner, self.shape
        return self.landed[stage - 1], (0, 0), self.landed[stage - 1].shape

    def link(self, stage):
        axis, first, second = self.order[stage]
        if first == second:
            return axis, first
        return axis, jnp.where(lax.rem(lax.axis_index("ctx"), 2) == 0, first, second)

    def spot(self, stage):
        axis, bit = self.link(stage)
        return bit_of(lax.axis_index(axis), bit)

    def copy(self, source, target, number, device):
        return pltpu.make_async_remote_copy(
            src_ref=source, dst_ref=target, send_sem=self.send.at[number],
            recv_sem=self.recv.at[number], device_id=device, device_id_type=MESH,
        )

    def outgoing(self, stage):
        ref, corner, shape = self.current(stage)
        if stage < self.plane:
            device = flipped(*self.link(stage))
            if stage < len(self.cuts):
                corner, shape = self.cut_at(corner, shape, self.cuts[stage], 1 - self.spot(stage))
        elif stage == self.plane or stage == self.count - 1:
            device = mirrored(2)
        else:
            device = mirrored(2 << (stage - self.plane))
        source = self.final if stage == self.count - 1 else self.view(ref, corner, shape)
        return self.copy(source, self.landed[stage], stage, device)

    def add(self, stage, target=None):
        ref, corner, shape = self.current(stage)
        if stage < len(self.cuts):
            corner, shape = self.cut_at(corner, shape, self.cuts[stage], self.spot(stage))
        landed = self.landed[stage]
        target = landed if target is None else target
        row, column = corner
        if not isinstance(column, int):
            column = pl.multiple_of(column, 128)
        take = next(rows for rows in (80, 48, 64, 32, 16) if shape[0] % rows == 0)

        def some(step, carry):
            at = step * take
            near = ref[pl.ds(pl.multiple_of(row + at, 16), take), pl.ds(column, shape[1])]
            here = pl.ds(pl.multiple_of(at, 16), take)
            both = near.astype(jnp.float32) + landed[here, :].astype(jnp.float32)
            target[here, :] = both.astype(jnp.bfloat16)
            return carry

        lax.fori_loop(0, shape[0] // take, some, 0)

    def share(self, depth):
        corner, shape = (0, 0), self.shape
        for stage in range(depth):
            corner, shape = self.cut_at(corner, shape, self.cuts[stage], self.spot(stage))
        return self.view(self.total, (corner[0] + self.corner[0], corner[1] + self.corner[1]), shape)

    def settle(self):
        return pltpu.make_async_copy(
            self.final, self.share(len(self.cuts)), self.send.at[self.count + len(self.cuts)]
        )

    def handing(self, back):
        stage = len(self.cuts) - 1 - back
        mine = self.share(stage + 1)
        return self.copy(
            self.final if back == 0 else mine, mine, self.count + back, flipped(*self.link(stage))
        )

    def run(self, op, inner):
        if op == 0:
            self.outgoing(0).start()
        elif op <= self.plane:
            self.outgoing(op - 1).wait_recv()
            self.add(op - 1)
            if op < self.plane:
                self.outgoing(op).start()
            else:
                @pl.when(jnp.logical_not(inner))
                def _():
                    self.outgoing(op).start()
        elif op < self.count:
            @pl.when(inner)
            def _():
                self.outgoing(op - 1).wait_recv()
                if op < self.count - 1:
                    self.add(op - 1)
                else:
                    self.add(op - 1, self.final)
                self.outgoing(op).start()
                if op == self.count - 1:
                    self.handing(0).start()
                    self.settle().start()
        elif op == self.count:
            @pl.when(jnp.logical_not(inner))
            def _():
                self.outgoing(op - 1).wait_recv()
                self.handing(0).start()
                self.settle().start()
        else:
            back = op - self.count - 1
            self.handing(back).wait_recv()
            if back == 0:
                self.settle().wait()
            if back + 1 < len(self.cuts):
                self.handing(back + 1).start()

    def drain(self, inner):
        for stage in range(self.plane):
            self.outgoing(stage).wait_send()

        @pl.when(inner)
        def _():
            for stage in range(self.plane + 1, self.count):
                self.outgoing(stage).wait_send()

        @pl.when(jnp.logical_not(inner))
        def _():
            self.outgoing(self.plane).wait_send()

        for back in range(len(self.cuts)):
            self.handing(back).wait_send()


RATES = {"core": 250e3, "dp": 85e3, "ctx": 42e3}
HOP_US = 2.0
STEP_US = 1.15
FEED_US = 3.0
OUT_US = 3.0
TAIL_US = 2.0


def planned(jobs, slots, relayed):
    work = []
    for plane, level_bits, cuts, size, _ in jobs:
        sizes = []
        for stage in range(plane):
            size = size / 2 if stage < len(cuts) else size
            sizes.append(("dp" if stage else "core", size))
        levels = [("ctx", size)] * (level_bits + 1)
        levels = [(name + str(number), size) for number, (name, size) in enumerate(levels)]
        work.append(sizes + levels + sizes[: len(cuts)][::-1])
    free, arrival, done, plan = {}, {}, [0] * len(jobs), []

    def issue(number, now):
        stage = done[number]
        if stage < len(work[number]):
            link, size = work[number][stage]
            free[link] = max(now, free.get(link, 0.0)) + size / RATES[link.rstrip("0123456789")]
            arrival[number] = free[link] + HOP_US
        done[number] += 1

    def live():
        return [n for n in range(len(jobs)) if 0 < done[n] <= len(work[n])]

    now = 0.0
    for slot, end in enumerate(slots):
        now = max(now, end)
        if slot in relayed:
            for link in ("ctx0", "ctx1"):
                free[link] = max(free.get(link, 0.0), now) + 2.2
        for number, job in enumerate(jobs):
            if job[4] == slot:
                plan.append((slot, number, 0))
                issue(number, now)
        for number in sorted((n for n in live() if arrival[n] <= now), key=lambda n: -done[n]):
            plan.append((slot, number, done[number]))
            now += 0.2
            issue(number, now)
    while live():
        number = min(live(), key=lambda n: (max(arrival[n] - now, 0.0), -done[n]))
        now = max(now, arrival[number]) + 0.2
        plan.append((len(slots), number, done[number]))
        issue(number, now)
    return plan


def greet(certain, perhaps):
    barrier = pltpu.get_barrier_semaphore()
    for target in certain:
        pl.semaphore_signal(barrier, inc=1, device_id=target, device_id_type=MESH)
    for target, there in perhaps:
        @pl.when(there)
        def _(target=target):
            pl.semaphore_signal(barrier, inc=1, device_id=target, device_id_type=MESH)


def await_peers(certain, perhaps):
    count = len(certain)
    for _, there in perhaps:
        count = count + there.astype(jnp.int32)
    pl.semaphore_wait(pltpu.get_barrier_semaphore(), count)


def before(ids, id_row):
    ids = ids[:1].astype(jnp.float32)
    first = jnp.zeros(id_row.shape, jnp.float32)
    for value in range(3):
        number = jnp.sum((ids == value).astype(jnp.float32), axis=1, keepdims=True)
        first += jnp.where(id_row > value, number, 0.0)
    return first.astype(jnp.int32)


def first_allowed(kv_ref, chip, id_row):
    return before(kv_ref[chip, pl.ds(0, ID_ROWS), :], id_row)


def first_in_half(kv_ref, chip, columns, id_row):
    return before(kv_ref[chip, pl.ds(0, ID_ROWS), columns], id_row)


def turn(values, cosine, sine_table):
    half_size = HEAD_DIM // 2
    first_half = values[:half_size]
    second_half = values[half_size:]
    return jnp.concatenate(
        [
            first_half * cosine - second_half * sine_table,
            second_half * cosine + first_half * sine_table,
        ],
        axis=0,
    )


def as_column(row):
    return jnp.broadcast_to(row, (8, row.shape[1])).T[:, :1]


def layer_kernel(
    order, level_bits, jobs, pumps, after,
    x_ref, id_ref, attn_gain_ref, ffn_gain_ref, cosine_in, sine_in, inverse_in,
    query_hbm, key_hbm, value_hbm, out_hbm, gate_hbm, up_hbm, down_hbm, cotangent_hbm,
    layer_out, input_grad, down_total, gate_total, up_total, out_total, query_total,
    kv_total,
    query_w, key_w, value_w, out_w, gate_w, up_w, down_w, cotangent_ref,
    kv, query_ref, query_pad, grad_ref, grad_pad, first_ref, normed_t, attended, acc, top,
    delta_ref, mixed_t, residual_t, unit_t, normed_grad, back, part, from_mate, from_above, turned_kv,
    turned_query, back_cosine, back_sine, turned_cotangent,
    down_part, gate_part, up_part, out_part, query_part, kv_part, lands,
    loads, up_send, below_recv, over_send, over_recv, mate_send, mate_recv, down_send, above_recv,
    sum_send, sum_recv,
):
    place = lax.axis_index("ctx")
    core, level = lax.rem(place, 2), lax.div(place, 2)
    levels, _, span = kv.shape
    rows = span // 2
    features = x_ref.shape[0]
    wide = gate_w.shape[1]
    count = KV_HEADS * levels
    mate = {"ctx": place + 1 - 2 * core}
    below = {"ctx": place - 2}
    above = {"ctx": place + 2}
    own = pl.ds(pl.multiple_of(core * rows, 128), rows)

    weights = [
        pltpu.make_async_copy(source, target, loads.at[number])
        for number, (source, target) in enumerate(
            (
                (key_hbm, key_w), (value_hbm, value_w), (query_hbm, query_w), (out_hbm, out_w),
                (gate_hbm, gate_w), (up_hbm, up_w), (down_hbm, down_w),
                (cotangent_hbm, cotangent_ref),
            )
        )
    ]
    for copy in weights:
        copy.start()

    carries = is_inner(level)
    side = 2 * bit_of(level, 1) - 1
    other = level + side
    certain = [flipped(axis, bit) for axis, bit, _ in order] + [mirrored(2)]
    perhaps = [({"ctx": place + 2 * side}, (other >= 0) & (other < levels))]
    perhaps += [(mirrored(2 << bit), carries) for bit in range(2, level_bits)]
    greet(certain, perhaps)

    sources = [(down_part, down_total), (gate_part, gate_total), (up_part, up_total)]
    places = [(*pair, (0, at)) for at in range(0, wide, FF_CHUNK) for pair in sources]
    places += [(out_part, out_total, (0, 0))]
    for head in range(KV_HEADS):
        places += [
            (query_part, query_total, (head * features, 0)),
            (kv_part, kv_total, (head * 2 * HEAD_DIM, 0)),
        ]
    streams = [
        Summed(
            order, level_bits, cuts, source, corner, shape, lands[number], total,
            sum_send.at[number], sum_recv.at[number],
        )
        for number, ((source, total, corner), (cuts, shape)) in enumerate(zip(places, jobs))
    ]

    def pump(slot):
        for number, op in pumps.get(slot, ()):
            streams[number].run(op, carries)

    x = x_ref[...].astype(jnp.float32)
    mean = jnp.sum(x * x, axis=0, keepdims=True) * (1.0 / features)
    inverse_attn = lax.rsqrt(mean + NORM_EPS)
    attn_gain = as_column(attn_gain_ref[...].reshape(1, features))
    normed_t[...] = (x * inverse_attn * attn_gain).astype(jnp.bfloat16)
    base = (place * rows).astype(jnp.float32) * inverse_in[...]
    base_cosine, base_sine = jnp.cos(base), jnp.sin(base)
    cosine = base_cosine * cosine_in[...] - base_sine * sine_in[...]
    sine_table = base_sine * cosine_in[...] + base_cosine * sine_in[...]
    kv[level, pl.ds(0, ID_ROWS), own] = jnp.broadcast_to(
        id_ref[...].astype(jnp.float32), (ID_ROWS, rows)
    ).astype(jnp.bfloat16)
    weights[0].wait()
    weights[1].wait()

    def piece_rows(head):
        if head == 0:
            return pl.ds(0, ID_ROWS + 2 * HEAD_DIM)
        return pl.ds(ID_ROWS + 2 * HEAD_DIM * head, 2 * HEAD_DIM)

    def upward(chip, head):
        return pltpu.make_async_remote_copy(
            src_ref=kv.at[chip, piece_rows(head), own], dst_ref=kv.at[chip, piece_rows(head), own],
            send_sem=up_send.at[chip, head], recv_sem=below_recv.at[chip, head],
            device_id=above, device_id_type=MESH,
        )

    def across(chip, head):
        return pltpu.make_async_remote_copy(
            src_ref=kv.at[chip, piece_rows(head), own], dst_ref=kv.at[chip, piece_rows(head), own],
            send_sem=over_send.at[chip, head], recv_sem=over_recv.at[chip, head],
            device_id=mate, device_id_type=MESH,
        )

    def hand_on(chip, head):
        @pl.when(level < levels - 1)
        def _():
            upward(chip, head).start()

        across(chip, head).start()

    keys = matmul(key_w[...], normed_t[...])
    values = matmul(value_w[...], normed_t[...])
    await_peers(certain, perhaps)
    for head in range(KV_HEADS):
        at = head * HEAD_DIM
        key = turn(keys[at : at + HEAD_DIM], cosine, sine_table)
        both = jnp.concatenate([key, values[at : at + HEAD_DIM]], axis=0)
        kv[level, pl.ds(ID_ROWS + 2 * at, 2 * HEAD_DIM), own] = both.astype(jnp.bfloat16)
        hand_on(level, head)
    weights[2].wait()
    queries = transposed_times(query_w[...], normed_t[...])
    scale = LOG2E / math.sqrt(HEAD_DIM)
    for head in range(KV_HEADS):
        for group in range(GROUPS):
            at = (head * GROUPS + group) * HEAD_DIM
            query = turn(queries[at : at + HEAD_DIM], cosine, sine_table) * scale
            query_ref[head, :, group * rows : (group + 1) * rows] = query.astype(jnp.bfloat16)
    nothing = jnp.zeros((HEAD_DIM, rows), jnp.bfloat16)
    for head in range(KV_HEADS):
        for group in range(GROUPS):
            piece = slice(group * rows, (group + 1) * rows)
            query_pad[head, piece, :] = jnp.concatenate(
                [query_ref[head, :, piece], nothing], axis=0
            ).T
    weights[7].wait()
    turned_cotangent[...] = cotangent_ref[...].T
    acc[...] = jnp.zeros_like(acc)
    top[...] = jnp.full_like(top, MASKED)
    id_row = jnp.concatenate([id_ref[...].astype(jnp.float32)] * GROUPS, axis=1)
    local = jnp.concatenate([lax.broadcasted_iota(jnp.int32, (1, rows), 1)] * GROUPS, axis=1)
    index = place * rows + local
    ones = jnp.ones((16, rows), jnp.bfloat16)

    def attend_block(chip, half, careful):
        begin = half * rows
        columns = pl.ds(pl.multiple_of(begin, 128), rows)
        first = first_ref[chip] - begin
        limit = index - chip * span - begin
        inside = first <= 0
        for head in range(KV_HEADS):
            key_at = ID_ROWS + 2 * HEAD_DIM * head
            key_t = kv[chip, pl.ds(key_at, HEAD_DIM), columns]
            value_t = kv[chip, pl.ds(key_at + HEAD_DIM, HEAD_DIM), columns]
            scores = transposed_times(key_t, query_ref[head])
            old = top[head]
            if careful:
                key_index = lax.broadcasted_iota(jnp.int32, scores.shape, 0)
                allowed = (key_index >= first) & (key_index <= limit)
                scores = jnp.where(allowed, scores, 2 * MASKED)
            new = jnp.maximum(old, jnp.max(scores, axis=0, keepdims=True))
            less = new
            if not careful:
                new = jnp.where(inside, new, old)
                less = jnp.where(inside, new, -MASKED)
            probs = jnp.exp2(scores - less).astype(jnp.bfloat16)
            acc[head] = acc[head] * jnp.exp2(old - new) + matmul(
                jnp.concatenate([value_t, ones], axis=0), probs
            )
            top[head] = new

    def one_block(turn_number, carry):
        chip, mates = level - lax.div(turn_number, 2), lax.rem(turn_number, 2)
        half = core + mates * (1 - 2 * core)
        block = 2 * chip + half

        @pl.when(chip >= 0)
        def _():
            for head in range(KV_HEADS):
                @pl.when((mates == 0) & (chip < level))
                def _(head=head):
                    upward(chip, head).wait_recv()
                    hand_on(chip, head)

                @pl.when(mates == 1)
                def _(head=head):
                    across(chip, head).wait_recv()

            @pl.when(mates == 1)
            def _():
                first_ref[chip] = first_allowed(kv, chip, id_row)

            @pl.when(mates == 0)
            def _():
                first_ref[chip] = first_in_half(kv, chip, own, id_row) + half * rows

            edge = (block == 0) | (block == place)

            @pl.when((block <= place) & edge)
            def _():
                attend_block(chip, half, True)

            @pl.when((block < place) & jnp.logical_not(edge))
            def _():
                attend_block(chip, half, False)

        return carry

    lax.fori_loop(0, 2 * levels, one_block, 0)
    for head in range(KV_HEADS):
        total = acc[head, HEAD_DIM : HEAD_DIM + 1, :]
        result = acc[head, :HEAD_DIM, :] * (1.0 / total)
        attended[head] = result
        top[head] = top[head] + jnp.log2(total)
        for group in range(GROUPS):
            at = (head * GROUPS + group) * HEAD_DIM
            piece = result[:, group * rows : (group + 1) * rows]
            mixed_t[pl.ds(at, HEAD_DIM), :] = piece.astype(jnp.bfloat16)

    for copy in weights[3:7]:
        copy.wait()
    residual = x_ref[...].astype(jnp.float32) + transposed_times(out_w[...], mixed_t[...])
    mean = jnp.sum(residual * residual, axis=0, keepdims=True) * (1.0 / features)
    inverse_ffn = lax.rsqrt(mean + NORM_EPS)
    ffn_gain = as_column(ffn_gain_ref[...].reshape(1, features))
    normed_ffn_t = (residual * inverse_ffn * ffn_gain).astype(jnp.bfloat16)
    normed_ffn = normed_ffn_t.T
    cotangent_t = cotangent_ref[...]
    cotangent = turned_cotangent[...]
    residual_t[...] = residual
    unit_t[...] = residual * inverse_ffn
    normed_grad[...] = jnp.zeros_like(normed_grad)
    for number, at in enumerate(range(0, wide, FF_CHUNK)):
        piece = slice(at, at + FF_CHUNK)
        gate = matmul(normed_ffn, gate_w[:, piece])
        up = matmul(normed_ffn, up_w[:, piece])
        sigmoid = 1.0 / (1.0 + jnp.exp(-gate))
        silu = gate * sigmoid
        hidden = (silu * up).astype(jnp.bfloat16)
        down_part[:, piece] = matmul(cotangent_t, hidden).astype(jnp.bfloat16)
        streams[3 * number].run(0, carries)
        grad_hidden = matmul(cotangent, down_w[:, piece])
        gate_grad = (grad_hidden * up * sigmoid * (1.0 + gate * (1.0 - sigmoid))).astype(
            jnp.bfloat16
        )
        up_grad = (grad_hidden * silu).astype(jnp.bfloat16)
        gate_part[:, piece] = matmul(normed_ffn_t, gate_grad).astype(jnp.bfloat16)
        streams[3 * number + 1].run(0, carries)
        up_part[:, piece] = matmul(normed_ffn_t, up_grad).astype(jnp.bfloat16)
        streams[3 * number + 2].run(0, carries)
        residual_t[...] += times_transposed(down_w[:, piece], hidden)
        normed_grad[...] += times_transposed(gate_w[:, piece], gate_grad) + times_transposed(
            up_w[:, piece], up_grad
        )
        pump(number)
    layer_out[...] = residual_t[...].astype(jnp.bfloat16)
    unit = unit_t[...]
    grad_normed = normed_grad[...]
    gain_grad = jnp.sum(grad_normed * unit, axis=1, keepdims=True)
    inner = grad_normed * ffn_gain
    mean = jnp.sum(inner * unit, axis=0, keepdims=True) * (1.0 / features)
    branch = cotangent_t.astype(jnp.float32) + inverse_ffn * (inner - unit * mean)
    residual_t[...] = branch
    branch = branch.astype(jnp.bfloat16)
    out_grads = times_transposed(mixed_t[...], branch)
    fill = jnp.broadcast_to(gain_grad, (features, out_part.shape[0] - features)).T
    out_part[:features, :] = out_grads.astype(jnp.bfloat16)
    out_part[features:, :] = fill.astype(jnp.bfloat16)
    chunks = wide // FF_CHUNK
    streams[3 * chunks].run(0, carries)
    mixed_grad = matmul(out_w[...], branch).astype(jnp.bfloat16)
    for head in range(KV_HEADS):
        for group in range(GROUPS):
            at = (head * GROUPS + group) * HEAD_DIM
            piece = slice(group * rows, (group + 1) * rows)
            grad = mixed_grad[at : at + HEAD_DIM, :]
            grad_ref[head, :, piece] = grad
            delta_ref[head, :, piece] = jnp.sum(
                grad.astype(jnp.float32) * attended[head, :, piece], axis=0, keepdims=True
            )
            grad_pad[head, piece, :] = jnp.concatenate([nothing, grad], axis=0).T
    pump(chunks)
    back[...] = jnp.zeros_like(back)

    def attend_back(step, half, careful):
        head = lax.div(step, levels)
        chip = lax.rem(step, levels)
        key_at = pl.multiple_of(ID_ROWS + 2 * HEAD_DIM * head, 16)
        value_at = pl.multiple_of(ID_ROWS + 2 * HEAD_DIM * head + HEAD_DIM, 16)
        begin = half * rows
        first = first_ref[chip] - begin
        limit = index - chip * span - begin
        less = top[head]
        if not careful:
            less = jnp.where(first <= 0, less, -MASKED)
        for at in range(0, rows, BACK_CHUNK):
            size = min(BACK_CHUNK, rows - at)
            columns = pl.ds(pl.multiple_of(begin + at, 128), size)
            key_t = kv[chip, pl.ds(key_at, HEAD_DIM), columns]
            value_t = kv[chip, pl.ds(value_at, HEAD_DIM), columns]
            scores = transposed_times(key_t, query_ref[head])
            if careful:
                key_index = at + lax.broadcasted_iota(jnp.int32, scores.shape, 0)
                allowed = (key_index >= first) & (key_index <= limit)
                scores = jnp.where(allowed, scores, MASKED)
            probs = jnp.exp2(scores - less)
            prob_grad = transposed_times(value_t, grad_ref[head])
            score_grad = (probs * (prob_grad - delta_ref[head])).astype(jnp.bfloat16)
            kv_back = matmul(score_grad, query_pad[head]) + matmul(
                probs.astype(jnp.bfloat16), grad_pad[head]
            )
            part[step, pl.ds(pl.multiple_of(begin + at, 128), size), :] = kv_back.astype(
                jnp.bfloat16
            )
            back[head] += matmul(key_t, score_grad)

    mate_rows = pl.ds(pl.multiple_of((1 - core) * rows, 128), rows)

    def to_mate(step):
        return pltpu.make_async_remote_copy(
            src_ref=part.at[step, mate_rows], dst_ref=from_mate.at[step],
            send_sem=mate_send.at[step], recv_sem=mate_recv.at[step],
            device_id=mate, device_id_type=MESH,
        )

    def to_below(step):
        return pltpu.make_async_remote_copy(
            src_ref=part.at[step, own], dst_ref=from_above.at[step],
            send_sem=down_send.at[step], recv_sem=above_recv.at[step],
            device_id=below, device_id_type=MESH,
        )

    def collect(step):
        chip = lax.rem(step, levels)
        to_mate(step).wait_recv()
        both = part[step, own, :].astype(jnp.float32) + from_mate[step].astype(jnp.float32)
        part[step, own, :] = both.astype(jnp.bfloat16)

        @pl.when(level < levels - 1)
        def _():
            to_below(step).wait_recv()
            more = part[step, own, :].astype(jnp.float32) + from_above[step].astype(jnp.float32)
            part[step, own, :] = more.astype(jnp.bfloat16)

        @pl.when(chip < level)
        def _():
            to_below(step).start()

    base = (place * rows).astype(jnp.float32) * inverse_in[...]
    base_cosine, base_sine = jnp.cos(base), -jnp.sin(base)
    back_cosine[...] = base_cosine * cosine_in[...] + base_sine * sine_in[...]
    back_sine[...] = base_sine * cosine_in[...] - base_cosine * sine_in[...]

    def head_done(head):
        cosine, sine_table = back_cosine[...], back_sine[...]
        step = head * levels + level
        both = part[step, own, :].astype(jnp.float32).T
        key_back = turn(both[:HEAD_DIM] * LN2, cosine, sine_table).astype(jnp.bfloat16)
        value_back = both[HEAD_DIM:].astype(jnp.bfloat16)
        kv_back = jnp.concatenate([key_back, value_back], axis=0)
        at = pl.multiple_of(head * 2 * HEAD_DIM, 2 * HEAD_DIM)
        turned_kv[pl.ds(at, 2 * HEAD_DIM), :] = kv_back
        kv_part[pl.ds(at, 2 * HEAD_DIM), :] = times_transposed(kv_back, normed_t[...]).astype(
            jnp.bfloat16
        )
        query_back = jnp.concatenate(
            [
                turn(
                    back[head, :, group * rows : (group + 1) * rows] * (1.0 / math.sqrt(HEAD_DIM)),
                    cosine, sine_table,
                ).astype(jnp.bfloat16)
                for group in range(GROUPS)
            ],
            axis=0,
        )
        wide_at = pl.multiple_of(head * GROUPS * HEAD_DIM, HEAD_DIM)
        turned_query[pl.ds(wide_at, GROUPS * HEAD_DIM), :] = query_back
        spare = jnp.zeros((features, QUERY_COLUMNS - GROUPS * HEAD_DIM), jnp.float32)
        query_part[pl.ds(pl.multiple_of(head * features, features), features), :] = jnp.concatenate(
            [times_transposed(normed_t[...], query_back), spare], axis=1
        ).astype(jnp.bfloat16)

    def one_step(turn_number, carry):
        step, own_turn = lax.div(turn_number, 2), lax.rem(turn_number, 2)
        half = core + (1 - own_turn) * (1 - 2 * core)
        chip = lax.rem(step, levels)
        block = 2 * chip + half

        @pl.when((step < count) & (chip <= level))
        def _():
            edge = (block == 0) | (block == place)

            @pl.when((block <= place) & edge)
            def _():
                attend_back(step, half, True)

            @pl.when((block < place) & jnp.logical_not(edge))
            def _():
                attend_back(step, half, False)

            @pl.when(block > place)
            def _():
                part[step, mate_rows, :] = jnp.zeros((rows, 2 * HEAD_DIM), jnp.bfloat16)

            @pl.when(own_turn == 0)
            def _():
                to_mate(step).start()

        due = step - levels + level

        @pl.when((own_turn == 1) & (due >= 0) & (due < count))
        def _():
            @pl.when(lax.rem(due, levels) <= level)
            def _():
                collect(due)

        ended = lax.div(step, levels) - 1

        @pl.when((own_turn == 1) & (step > 0) & (lax.rem(step, levels) == 0))
        def _():
            head_done(ended)
            for head in range(KV_HEADS):
                @pl.when(ended == head)
                def _(head=head):
                    if head < KV_HEADS - 1:
                        streams[3 * chunks + 1 + 2 * head].run(0, carries)
                    streams[3 * chunks + 2 + 2 * head].run(0, carries)

        for slot in sorted(pumps):
            if slot > chunks:
                @pl.when(turn_number == slot - chunks - 1)
                def _(slot=slot):
                    pump(slot)

        return carry

    lax.fori_loop(0, 2 * (count + 1), one_step, 0)

    grad_t = matmul(query_w[...], turned_query[...])
    for head in range(KV_HEADS):
        at = head * HEAD_DIM
        weight = jnp.concatenate(
            [key_w[at : at + HEAD_DIM, :], value_w[at : at + HEAD_DIM, :]], axis=0
        )
        grad_t += transposed_times(weight, turned_kv[2 * at : 2 * at + 2 * HEAD_DIM, :])
    x = x_ref[...].astype(jnp.float32)
    mean = jnp.sum(x * x, axis=0, keepdims=True) * (1.0 / features)
    inverse_attn = lax.rsqrt(mean + NORM_EPS)
    unit = x * inverse_attn
    gain_column = jnp.sum(grad_t * unit, axis=1, keepdims=True)
    last_rows = slice((KV_HEADS - 1) * features, KV_HEADS * features)
    last = query_part[last_rows, QUERY_COLUMNS - 128 :].astype(jnp.float32)
    spare = lax.broadcasted_iota(jnp.int32, last.shape, 1) >= HEAD_DIM
    query_part[last_rows, QUERY_COLUMNS - 128 :] = jnp.where(spare, gain_column, last).astype(
        jnp.bfloat16
    )
    streams[3 * chunks + 2 * KV_HEADS - 1].run(0, carries)
    inner = grad_t * as_column(attn_gain_ref[...].reshape(1, features))
    mean = jnp.sum(inner * unit, axis=0, keepdims=True) * (1.0 / features)
    input_grad[...] = (residual_t[...] + inverse_attn * (inner - unit * mean)).astype(jnp.bfloat16)
    for number, op in after:
        streams[number].run(op, carries)
    for stream in streams:
        stream.drain(carries)

    def ended(step, carry):
        chip = lax.rem(step, levels)

        @pl.when(chip <= level)
        def _():
            to_mate(step).wait_send()

        @pl.when(chip < level)
        def _():
            to_below(step).wait_send()

        return carry

    lax.fori_loop(0, count, ended, 0)

    def handed_on(chip, carry):
        @pl.when(chip <= level)
        def _():
            for head in range(KV_HEADS):
                across(chip, head).wait_send()

                @pl.when(level < levels - 1)
                def _(head=head):
                    upward(chip, head).wait_send()

        return carry

    lax.fori_loop(0, levels, handed_on, 0)


def rotary_tables(rows):
    half_size = HEAD_DIM // 2
    inverse = (ROPE_BASE ** (-np.arange(half_size, dtype=np.float64) * 2.0 / HEAD_DIM))[:, None]
    phase = inverse * np.arange(rows, dtype=np.float64)[None, :]
    return tuple(
        jnp.asarray(table, jnp.float32) for table in (np.cos(phase), np.sin(phase), inverse)
    )


def layer(x_t, ids, attn_gain, ffn_gain, w_query, w_key_t, w_value_t, w_out, w_gate, w_up,
          w_down_t, cotangent_t):
    dp_count, ctx_count = lax.axis_size("dp"), lax.axis_size("ctx")
    order = plane_order(dp_count)
    level_bits = (ctx_count // 2).bit_length() - 1
    levels = ctx_count // 2
    features, rows = x_t.shape
    wide = w_gate.shape[1]
    span, queries = 2 * rows, GROUPS * rows
    count = KV_HEADS * levels
    chunks = wide // FF_CHUNK

    heads = [("rrc", (features, QUERY_COLUMNS)), ("rrr", (2 * HEAD_DIM, features))] * KV_HEADS
    jobs = [("rrc", (features, FF_CHUNK))] * (3 * chunks) + [("rrr", (OUT_ROWS, features))] + heads
    slots = [FEED_US * number for number in range(chunks)]
    slots.append(slots[-1] + OUT_US)
    turns = 2 * (count + 1)
    slots += [slots[-1] + STEP_US * (number + 1) for number in range(turns)]
    slots.append(slots[-1] + TAIL_US)
    begins = [number // 3 for number in range(3 * chunks)] + [chunks]
    for head in range(KV_HEADS):
        begins += [chunks + 2 * (head + 1) * levels + 2] * 2
    begins[-2] = len(slots) - 1
    relayed = [
        chunks + 2 + 2 * step for step in range(count) if step % levels < levels - 1
    ]
    pumps, after = {}, []
    for slot, number, op in planned(
        [
            (len(order), level_bits, cuts, 2 * shape[0] * shape[1], begin)
            for (cuts, shape), begin in zip(jobs, begins)
        ],
        slots, relayed,
    ):
        if op == 0:
            continue
        if slot <= chunks + turns:
            pumps.setdefault(slot, []).append((number, op))
        else:
            after.append((number, op))

    vmem = lambda shape, dtype=jnp.bfloat16: pltpu.VMEM(shape, dtype)
    lands = [
        [vmem(size) for size in landing_shapes(*shape, cuts, len(order), level_bits)]
        for cuts, shape in jobs
    ]
    dma = lambda *shape: pltpu.SemaphoreType.DMA(shape)
    semaphores = len(order) + level_bits + HALVINGS + 2
    head_t = (KV_HEADS, HEAD_DIM, queries)
    padded = (KV_HEADS, queries, 2 * HEAD_DIM)
    row = (KV_HEADS, 1, queries)
    f32 = jnp.float32
    totals = [(features, wide)] * 3 + [(OUT_ROWS, features)]
    totals += [(KV_HEADS * features, QUERY_COLUMNS), (2 * KV_HEADS * HEAD_DIM, features)]
    anywhere = pl.BlockSpec(memory_space=pl.ANY)
    return pl.pallas_call(
        functools.partial(layer_kernel, order, level_bits, jobs, pumps, after),
        out_shape=tuple(
            jax.ShapeDtypeStruct(shape, jnp.bfloat16) for shape in [(features, rows)] * 2 + totals
        ),
        in_specs=in_vmem(7) + [anywhere] * 8,
        out_specs=tuple(in_vmem(2) + [anywhere] * 6),
        scratch_shapes=[
            vmem(w_query.shape), vmem(w_key_t.shape), vmem(w_value_t.shape), vmem(w_out.shape),
            vmem(w_gate.shape), vmem(w_up.shape), vmem(w_down_t.shape), vmem((features, rows)),
            vmem((levels, ID_ROWS + 2 * KV_HEADS * HEAD_DIM, span)),
            vmem(head_t), vmem(padded), vmem(head_t), vmem(padded),
            vmem((levels, 1, queries), jnp.int32),
            vmem((features, rows)),
            vmem(head_t, f32),
            vmem((KV_HEADS, HEAD_DIM + 16, queries), f32),
            vmem(row, f32), vmem(row, f32),
            vmem((features, rows)),
            *[vmem((features, rows), f32) for _ in range(3)],
            vmem(head_t, f32),
            vmem((count, span, 2 * HEAD_DIM)),
            vmem((count, rows, 2 * HEAD_DIM)), vmem((count, rows, 2 * HEAD_DIM)),
            vmem((2 * KV_HEADS * HEAD_DIM, rows)), vmem((HEADS * HEAD_DIM, rows)),
            vmem((HEAD_DIM // 2, rows), f32), vmem((HEAD_DIM // 2, rows), f32),
            vmem((rows, features)),
            *[vmem(shape) for shape in totals],
            lands,
            dma(8),
            *[dma(levels, KV_HEADS) for _ in range(4)],
            *[dma(count) for _ in range(4)],
            dma(len(jobs), semaphores), dma(len(jobs), semaphores),
        ],
        compiler_params=pltpu.CompilerParams(
            collective_id=1, has_side_effects=True, vmem_limit_bytes=60 * 1024 * 1024
        ),
        name="layer",
    )(
        x_t, ids, attn_gain, ffn_gain, *rotary_tables(rows), w_query, w_key_t, w_value_t, w_out,
        w_gate, w_up, w_down_t, cotangent_t,
    )


PIECES = 2
SOME_ROWS = 48


def finish_kernel(
    layer_in, input_in, gate, up, down_t, out, query, kv,
    layer_out, input_out, gate_out, up_out, down_out, out_out, key_out, value_out, query_out,
    gain_ffn, gain_attn,
    held, made, out_held, out_made, query_held, query_made, kv_held, key_made, value_made, passed,
    come, go,
):
    features = gate.shape[0]
    piece = features // PIECES
    passed_in = [
        pltpu.make_async_copy(source, passed.at[number], come.at[3 * PIECES + 3 + number])
        for number, source in enumerate((layer_in, input_in))
    ]
    passed_out = [
        pltpu.make_async_copy(passed.at[number], target, go.at[number])
        for number, target in enumerate((layer_out, input_out))
    ]
    wide = []
    for source, target in ((gate, gate_out), (up, up_out), (down_t, down_out)):
        for number in range(PIECES):
            rows, at = pl.ds(number * piece, piece), len(wide)
            wide.append(
                (
                    pltpu.make_async_copy(source.at[rows], held.at[at], come.at[at]),
                    pltpu.make_async_copy(made.at[at], target.at[rows], go.at[2 + at]),
                )
            )
    at = len(wide)
    small_in = [
        pltpu.make_async_copy(source, target, come.at[at + number])
        for number, (source, target) in enumerate(
            ((out, out_held), (query, query_held), (kv, kv_held))
        )
    ]
    small_out = [
        pltpu.make_async_copy(source, target, go.at[2 + at + number])
        for number, (source, target) in enumerate(
            (
                (out_made, out_out), (query_made, query_out), (key_made, key_out),
                (value_made, value_out),
            )
        )
    ]
    for arrival, _ in wide:
        arrival.start()
    for copy in small_in + passed_in:
        copy.start()

    def by_rows(count, convert):
        def some(step, carry):
            convert(pl.ds(pl.multiple_of(step * SOME_ROWS, 16), SOME_ROWS), step * SOME_ROWS)
            return carry

        lax.fori_loop(0, count // SOME_ROWS, some, 0)

    for at, (arrival, departure) in enumerate(wide):
        arrival.wait()

        def convert(rows, start, at=at):
            made[at, rows, :] = held[at, rows, :].astype(jnp.float32)

        by_rows(piece, convert)
        departure.start()

    small_in[0].wait()

    def convert_out(rows, start):
        out_made[rows, :] = out_held[rows, :].astype(jnp.float32)

    by_rows(features, convert_out)
    small_out[0].start()
    gain_ffn[...] = out_held[OUT_ROWS - 16 :, :].astype(jnp.float32)[-1]
    small_in[1].wait()
    width = GROUPS * HEAD_DIM

    def convert_query(rows, start):
        query_made[rows, :] = jnp.concatenate(
            [
                query_held[
                    pl.ds(pl.multiple_of(head * features + start, 16), SOME_ROWS), :
                ].astype(jnp.float32)[:, :width]
                for head in range(KV_HEADS)
            ],
            axis=1,
        )

    by_rows(features, convert_query)
    small_out[1].start()
    last = query_held[(KV_HEADS - 1) * features :, QUERY_COLUMNS - 128 :].astype(jnp.float32)
    gain_attn[...] = last.T[-1]
    small_in[2].wait()
    for head in range(KV_HEADS):
        at = head * HEAD_DIM
        key_made[at : at + HEAD_DIM, :] = kv_held[2 * at : 2 * at + HEAD_DIM, :].astype(jnp.float32)
        value_made[at : at + HEAD_DIM, :] = kv_held[
            2 * at + HEAD_DIM : 2 * at + 2 * HEAD_DIM, :
        ].astype(jnp.float32)
    small_out[2].start()
    small_out[3].start()
    for arrival, departure in zip(passed_in, passed_out):
        arrival.wait()
        departure.start()
    for copy in passed_out + [departure for _, departure in wide] + small_out:
        copy.wait()


def finish(layer_t, input_t, down_t, gate, up, out, query, kv):
    features, wide = gate.shape
    key_width = KV_HEADS * HEAD_DIM
    f32 = jnp.float32
    anywhere = pl.BlockSpec(memory_space=pl.ANY)
    shape = lambda *dims: jax.ShapeDtypeStruct(dims, f32)
    short = jax.ShapeDtypeStruct(layer_t.shape, layer_t.dtype)
    vmem = lambda *dims: pltpu.VMEM(dims, jnp.bfloat16)
    vmem_f32 = lambda *dims: pltpu.VMEM(dims, f32)
    copies = 3 * PIECES
    return pl.pallas_call(
        finish_kernel,
        out_shape=(
            short, short,
            shape(features, wide), shape(features, wide), shape(features, wide),
            shape(features, features), shape(key_width, features), shape(key_width, features),
            shape(features, features), shape(features), shape(features),
        ),
        in_specs=[anywhere] * 8,
        out_specs=tuple([anywhere] * 9 + in_vmem(2)),
        scratch_shapes=[
            vmem(copies, features // PIECES, wide), vmem_f32(copies, features // PIECES, wide),
            vmem(OUT_ROWS, features), vmem_f32(features, features),
            vmem(*query.shape), vmem_f32(features, features),
            vmem(*kv.shape), vmem_f32(key_width, features), vmem_f32(key_width, features),
            vmem(2, *layer_t.shape),
            pltpu.SemaphoreType.DMA((copies + 5,)), pltpu.SemaphoreType.DMA((copies + 6,)),
        ],
        compiler_params=pltpu.CompilerParams(vmem_limit_bytes=60 * 1024 * 1024),
        name="finish",
    )(layer_t, input_t, gate, up, down_t, out, query, kv)


def in_vmem(count):
    return [pl.BlockSpec(memory_space=pltpu.VMEM)] * count


def on_device(
    hidden_in, segment_ids, w_query, w_key, w_value, w_out, w_gate, w_up, w_down, gain_attn,
    gain_ffn, out_grad,
):
    summed = layer(
        hidden_in[0].T, segment_ids, gain_attn, gain_ffn, w_query, w_key.T, w_value.T,
        w_out, w_gate, w_up, w_down.T, out_grad[0].T,
    )
    (
        layer_t, input_t, grad_gate, grad_up, grad_down_t, grad_out, grad_key_t, grad_value_t,
        grad_query, grad_gain_ffn, grad_gain_attn,
    ) = finish(*summed)
    return (
        layer_t.T[None], input_t.T[None], grad_query, grad_key_t.T, grad_value_t.T, grad_out,
        grad_gate, grad_up, grad_down_t.T, grad_gain_attn, grad_gain_ffn,
    )


def solution(mesh):
    rows = P("dp", "ctx", None)
    return jax.shard_map(
        on_device,
        mesh=mesh,
        in_specs=(rows, P("dp", "ctx")) + (P(),) * 9 + (rows,),
        out_specs=(rows, rows) + (P(),) * 9,
        check_vma=False,
    )
```

```python
import functools
import math

import jax
import jax.numpy as jnp
import numpy as np
from jax import lax
from jax.experimental import pallas as pl
from jax.experimental.pallas import tpu as pltpu
from jax.sharding import PartitionSpec as P

HEADS = 9
KV_HEADS = 3
HEAD_DIM = 64
GROUPS = HEADS // KV_HEADS

NORM_EPS = 1e-05
ROPE_BASE = 10000.0
MASKED = -1e30
LOG2E = 1.4426950408889634
LN2 = 0.6931471805599453
MESH = pl.DeviceIdType.MESH
OUT_ROWS = 640
QUERY_COLUMNS = 256
ID_ROWS = 16
CHUNK = 256
FF_CHUNK = 512
BACK_CHUNK = 384


def matmul(left_side, right_side):
    return jnp.dot(left_side, right_side, preferred_element_type=jnp.float32)


def times_transposed(left_side, right_side):
    return lax.dot_general(
        left_side, right_side, (((1,), (1,)), ((), ())), preferred_element_type=jnp.float32
    )


def transposed_times(left_side, right_side):
    return lax.dot_general(
        left_side, right_side, (((0,), (0,)), ((), ())), preferred_element_type=jnp.float32
    )


def bit_of(place, bit):
    return lax.rem(lax.div(place, bit), 2)


def plane_order(dp_count):
    bits = [1 << i for i in range(dp_count.bit_length() - 1)]
    return [("ctx", 1, 1)] + [("dp", bit, bits[(i + 1) % len(bits)]) for i, bit in enumerate(bits)]


def sum_links(order, level_bits, slice_place, place):
    core, level = lax.rem(place, 2), lax.div(place, 2)
    picks, devices = [], []
    for axis, first, second in order:
        at = slice_place if axis == "dp" else place
        pick, bit = bit_of(at, first), first
        if second != first:
            pick = jnp.where(core == 0, pick, bit_of(at, second))
            bit = jnp.where(core == 0, first, second)
        partner = at + (1 - 2 * pick) * bit
        picks.append(pick)
        devices.append((partner, place) if axis == "dp" else (slice_place, partner))
    mirrors = []
    for number in range(level_bits):
        size = 2 << number
        group = lax.div(level, size) * size
        mirrors.append((slice_place, 2 * (2 * group + size - 1 - level) + core))
    return picks, devices, mirrors


def crossed_order(order, ctx_count):
    bits = [1 << i for i in range(1, ctx_count.bit_length() - 1)]
    return order + [("ctx", bit, bits[(i + 1) % len(bits)]) for i, bit in enumerate(bits)]


def is_inner(level):
    return lax.rem(level, 2) != lax.rem(lax.div(level, 2), 2)


HALVINGS = 3
SLOTS = 5


def halved_shapes(rows, columns, cuts):
    shapes = []
    for cut in cuts:
        rows, columns = (rows // 2, columns) if cut == "r" else (rows, columns // 2)
        shapes.append((rows, columns))
    return shapes


def landing_shapes(rows, columns, cuts, plane, level_bits):
    shapes = halved_shapes(rows, columns, cuts)
    last = shapes[-1] if shapes else (rows, columns)
    return shapes + [last] * (plane - len(cuts) + (level_bits + 1 if level_bits else 0))


class Summed:
    def __init__(self, links, level_bits, cuts, source, corner, shape, landed, total, send, recv):
        self.picks, self.devices, self.mirrors = links
        self.level_bits, self.cuts = level_bits, cuts
        self.landed, self.total = landed, total
        self.source, self.corner, self.shape = source, corner, shape
        self.send, self.recv = send, recv
        self.plane = len(self.picks)
        self.count = self.plane + (level_bits + 1 if level_bits else 0)
        self.final = landed[-1]

    def cut_at(self, corner, shape, cut, pick):
        rows, columns = shape
        row, column = corner
        if cut == "r":
            rows //= 2
            row = row + pick * rows
        else:
            columns //= 2
            column = column + pick * columns
        return (row, column), (rows, columns)

    @staticmethod
    def view(ref, corner, shape):
        row, column = corner
        if not isinstance(row, int):
            row = pl.multiple_of(row, 16)
        if not isinstance(column, int):
            column = pl.multiple_of(column, 128)
        return ref.at[pl.ds(row, shape[0]), pl.ds(column, shape[1])]

    def current(self, stage):
        if stage == 0:
            return self.source, self.corner, self.shape
        return self.landed[stage - 1], (0, 0), self.landed[stage - 1].shape

    def copy(self, source, target, number, device):
        return pltpu.make_async_remote_copy(
            src_ref=source, dst_ref=target, send_sem=self.send.at[number],
            recv_sem=self.recv.at[number], device_id=device, device_id_type=MESH,
        )

    def outgoing(self, stage):
        ref, corner, shape = self.current(stage)
        if stage < self.plane:
            device = self.devices[stage]
            if stage < len(self.cuts):
                corner, shape = self.cut_at(corner, shape, self.cuts[stage], 1 - self.picks[stage])
        elif stage == self.plane or stage == self.count - 1:
            device = self.mirrors[0]
        else:
            device = self.mirrors[stage - self.plane]
        given = self.level_bits and stage == self.count - 1
        source = self.final if given else self.view(ref, corner, shape)
        return self.copy(source, self.landed[stage], stage, device)

    def add(self, stage, target=None):
        ref, corner, shape = self.current(stage)
        if stage < len(self.cuts):
            corner, shape = self.cut_at(corner, shape, self.cuts[stage], self.picks[stage])
        landed = self.landed[stage]
        target = landed if target is None else target
        row, column = corner
        if not isinstance(column, int):
            column = pl.multiple_of(column, 128)
        take = next(rows for rows in (80, 48, 64, 32, 16) if shape[0] % rows == 0)

        def some(step, carry):
            at = step * take
            near = ref[pl.ds(pl.multiple_of(row + at, 16), take), pl.ds(column, shape[1])]
            here = pl.ds(pl.multiple_of(at, 16), take)
            both = near.astype(jnp.float32) + landed[here, :].astype(jnp.float32)
            target[here, :] = both.astype(jnp.bfloat16)
            return carry

        lax.fori_loop(0, shape[0] // take, some, 0)

    def share(self, depth):
        corner, shape = (0, 0), self.shape
        for stage in range(depth):
            corner, shape = self.cut_at(corner, shape, self.cuts[stage], self.picks[stage])
        return self.view(self.total, (corner[0] + self.corner[0], corner[1] + self.corner[1]), shape)

    def settle(self):
        return pltpu.make_async_copy(
            self.final, self.share(len(self.cuts)), self.send.at[self.count + len(self.cuts)]
        )

    def handing(self, back):
        stage = len(self.cuts) - 1 - back
        mine = self.share(stage + 1)
        return self.copy(
            self.final if back == 0 else mine, mine, self.count + back, self.devices[stage]
        )

    def run(self, op, inner):
        if op == 0:
            self.outgoing(0).start()
        elif op <= self.plane:
            self.outgoing(op - 1).wait_recv()
            self.add(op - 1)
            if op < self.plane:
                self.outgoing(op).start()
            elif not self.level_bits:
                self.settle().start()
                if self.cuts:
                    self.handing(0).start()
                else:
                    self.settle().wait()
            else:
                @pl.when(jnp.logical_not(inner))
                def _():
                    self.outgoing(op).start()
        elif op < self.count:
            @pl.when(inner)
            def _():
                self.outgoing(op - 1).wait_recv()
                if op < self.count - 1:
                    self.add(op - 1)
                else:
                    self.add(op - 1, self.final)
                self.outgoing(op).start()
                if op == self.count - 1:
                    self.handing(0).start()
                    self.settle().start()
        elif op == self.count:
            @pl.when(jnp.logical_not(inner))
            def _():
                self.outgoing(op - 1).wait_recv()
                self.handing(0).start()
                self.settle().start()
        else:
            back = op - self.count - 1
            self.handing(back).wait_recv()
            if back == 0:
                self.settle().wait()
            if back + 1 < len(self.cuts):
                self.handing(back + 1).start()

    def drain(self, inner):
        for stage in range(self.plane):
            self.outgoing(stage).wait_send()

        if self.level_bits:
            @pl.when(inner)
            def _():
                for stage in range(self.plane + 1, self.count):
                    self.outgoing(stage).wait_send()

            @pl.when(jnp.logical_not(inner))
            def _():
                self.outgoing(self.plane).wait_send()

        for back in range(len(self.cuts)):
            self.handing(back).wait_send()


RATES = {"core": 250e3, "dp": 85e3, "ctx": 42e3}
HOP_US = 2.0
STEP_US = 1.15
FEED_US = 3.0
OUT_US = 3.0
TAIL_US = 2.0


def planned(jobs, slots, relayed):
    work = []
    for plane, crossed, level_bits, cuts, size, _ in jobs:
        sizes = []
        for stage in range(plane):
            size = size / 2 if stage < len(cuts) else size
            sizes.append(("dp" if stage else "core", size))
        levels = [("ctx", size)] * (crossed if crossed else level_bits + 1)
        levels = [(name + str(number), size) for number, (name, size) in enumerate(levels)]
        work.append(sizes + levels + sizes[: len(cuts)][::-1])
    free, arrival, done, plan = {}, {}, [0] * len(jobs), []

    def issue(number, now):
        stage = done[number]
        if stage < len(work[number]):
            link, size = work[number][stage]
            free[link] = max(now, free.get(link, 0.0)) + size / RATES[link.rstrip("0123456789")]
            arrival[number] = free[link] + HOP_US
        done[number] += 1

    def live():
        return [n for n in range(len(jobs)) if 0 < done[n] <= len(work[n])]

    now = 0.0
    for slot, end in enumerate(slots):
        now = max(now, end)
        if slot in relayed:
            for link in ("ctx0", "ctx1"):
                free[link] = max(free.get(link, 0.0), now) + 2.2
        for number, job in enumerate(jobs):
            if job[5] == slot:
                plan.append((slot, number, 0))
                issue(number, now)
        for number in sorted((n for n in live() if arrival[n] <= now), key=lambda n: -done[n]):
            plan.append((slot, number, done[number]))
            now += 0.2
            issue(number, now)
    while live():
        number = min(live(), key=lambda n: (max(arrival[n] - now, 0.0), -done[n]))
        now = max(now, arrival[number]) + 0.2
        plan.append((len(slots), number, done[number]))
        issue(number, now)
    return plan


def greet(certain, perhaps):
    barrier = pltpu.get_barrier_semaphore()
    for target in certain:
        pl.semaphore_signal(barrier, inc=1, device_id=target, device_id_type=MESH)
    for target, there in perhaps:
        @pl.when(there)
        def _(target=target):
            pl.semaphore_signal(barrier, inc=1, device_id=target, device_id_type=MESH)


def await_peers(certain, perhaps):
    count = len(certain)
    for _, there in perhaps:
        count = count + there.astype(jnp.int32)
    pl.semaphore_wait(pltpu.get_barrier_semaphore(), count)


def before(ids, id_row):
    ids = ids[:1].astype(jnp.float32)
    first = jnp.zeros(id_row.shape, jnp.float32)
    for value in range(3):
        number = jnp.sum((ids == value).astype(jnp.float32), axis=1, keepdims=True)
        first += jnp.where(id_row > value, number, 0.0)
    return first.astype(jnp.int32)


def first_allowed(kv_ref, chip, id_row):
    return before(kv_ref[chip, pl.ds(0, ID_ROWS), :], id_row)


def first_in_half(kv_ref, chip, columns, id_row):
    return before(kv_ref[chip, pl.ds(0, ID_ROWS), columns], id_row)


def turn(values, cosine, sine_table):
    half_size = HEAD_DIM // 2
    first_half = values[:half_size]
    second_half = values[half_size:]
    return jnp.concatenate(
        [
            first_half * cosine - second_half * sine_table,
            second_half * cosine + first_half * sine_table,
        ],
        axis=0,
    )


def as_column(row):
    return jnp.broadcast_to(row, (8, row.shape[1])).T[:, :1]


def layer_kernel(
    order, crossed, level_bits, jobs, pumps, after,
    x_ref, id_ref, attn_gain_ref, ffn_gain_ref, cosine_in, sine_in, inverse_in,
    query_hbm, key_hbm, value_hbm, out_hbm, gate_hbm, up_hbm, down_hbm, cotangent_hbm,
    layer_out, input_grad, down_total, gate_total, up_total, out_total, query_total,
    kv_total, gain_total,
    query_w, key_w, value_w, out_w, gate_w, up_w, down_w, cotangent_ref,
    kv, query_ref, query_pad, grad_ref, grad_pad, first_ref, normed_t, attended, acc, top,
    delta_ref, mixed_t, residual_t, unit_t, normed_grad, back, part, from_mate, from_above, turned_kv,
    turned_query, back_cosine, back_sine, turned_cotangent,
    down_part, gate_part, up_part, out_part, query_part, kv_part, gain_part, lands,
    loads, up_send, below_recv, over_send, over_recv, mate_send, mate_recv, down_send, above_recv,
    sum_send, sum_recv,
):
    place = lax.axis_index("ctx")
    core, level = lax.rem(place, 2), lax.div(place, 2)
    levels, _, span = kv.shape
    rows = span // 2
    features = x_ref.shape[0]
    wide = gate_w.shape[1]
    count = KV_HEADS * levels
    slice_place = lax.axis_index("dp")
    mate = (slice_place, place + 1 - 2 * core)
    below = (slice_place, place - 2)
    above = (slice_place, place + 2)
    links = {
        True: sum_links(order, level_bits, slice_place, place),
        False: sum_links(crossed, 0, slice_place, place),
    }
    own = pl.ds(pl.multiple_of(core * rows, 128), rows)

    weights = [
        pltpu.make_async_copy(source, target, loads.at[number])
        for number, (source, target) in enumerate(
            (
                (key_hbm, key_w), (value_hbm, value_w), (query_hbm, query_w), (out_hbm, out_w),
                (gate_hbm, gate_w), (up_hbm, up_w), (down_hbm, down_w),
                (cotangent_hbm, cotangent_ref),
            )
        )
    ]
    for copy in weights:
        copy.start()

    carries = is_inner(level)
    side = 2 * bit_of(level, 1) - 1
    other = level + side
    certain = links[False][1]
    perhaps = [((slice_place, place + 2 * side), (other >= 0) & (other < levels))]
    perhaps += [(device, carries) for device in links[True][2][2:]]
    greet(certain, perhaps)

    sources = [(down_part, down_total), (gate_part, gate_total), (up_part, up_total)]
    places = [(*pair, (0, at)) for at in range(0, wide, FF_CHUNK) for pair in sources]
    places += [(out_part, out_total, (0, 0))]
    for head in range(KV_HEADS):
        places += [
            (query_part, query_total, (head * features, 0)),
            (kv_part, kv_total, (head * 2 * HEAD_DIM, 0)),
        ]
    places += [(gain_part, gain_total, (0, 0))]
    streams = [
        Summed(
            links[folded], level_bits if folded else 0, cuts, source, corner, shape, lands[number], total,
            sum_send.at[number], sum_recv.at[number],
        )
        for number, ((source, total, corner), (folded, cuts, shape)) in enumerate(zip(places, jobs))
    ]

    def pump(slot):
        for number, op in pumps.get(slot, ()):
            streams[number].run(op, carries)

    x = x_ref[...].astype(jnp.float32)
    mean = jnp.sum(x * x, axis=0, keepdims=True) * (1.0 / features)
    inverse_attn = lax.rsqrt(mean + NORM_EPS)
    attn_gain = as_column(attn_gain_ref[...].reshape(1, features))
    normed_t[...] = (x * inverse_attn * attn_gain).astype(jnp.bfloat16)
    base = (place * rows).astype(jnp.float32) * inverse_in[...]
    base_cosine, base_sine = jnp.cos(base), jnp.sin(base)
    cosine = base_cosine * cosine_in[...] - base_sine * sine_in[...]
    sine_table = base_sine * cosine_in[...] + base_cosine * sine_in[...]
    kv[level, pl.ds(0, ID_ROWS), own] = jnp.broadcast_to(
        id_ref[...].astype(jnp.float32), (ID_ROWS, rows)
    ).astype(jnp.bfloat16)
    weights[0].wait()
    weights[1].wait()

    def piece_rows(head):
        if head == 0:
            return pl.ds(0, ID_ROWS + 2 * HEAD_DIM)
        return pl.ds(ID_ROWS + 2 * HEAD_DIM * head, 2 * HEAD_DIM)

    def upward(chip, head):
        return pltpu.make_async_remote_copy(
            src_ref=kv.at[chip, piece_rows(head), own], dst_ref=kv.at[chip, piece_rows(head), own],
            send_sem=up_send.at[chip, head], recv_sem=below_recv.at[chip, head],
            device_id=above, device_id_type=MESH,
        )

    def across(chip, head):
        return pltpu.make_async_remote_copy(
            src_ref=kv.at[chip, piece_rows(head), own], dst_ref=kv.at[chip, piece_rows(head), own],
            send_sem=over_send.at[chip, head], recv_sem=over_recv.at[chip, head],
            device_id=mate, device_id_type=MESH,
        )

    def hand_on(chip, head):
        @pl.when(level < levels - 1)
        def _():
            upward(chip, head).start()

        across(chip, head).start()

    keys = matmul(key_w[...], normed_t[...])
    values = matmul(value_w[...], normed_t[...])
    await_peers(certain, perhaps)
    for head in range(KV_HEADS):
        at = head * HEAD_DIM
        key = turn(keys[at : at + HEAD_DIM], cosine, sine_table)
        both = jnp.concatenate([key, values[at : at + HEAD_DIM]], axis=0)
        kv[level, pl.ds(ID_ROWS + 2 * at, 2 * HEAD_DIM), own] = both.astype(jnp.bfloat16)
        hand_on(level, head)
    weights[2].wait()
    queries = transposed_times(query_w[...], normed_t[...])
    scale = LOG2E / math.sqrt(HEAD_DIM)
    for head in range(KV_HEADS):
        for group in range(GROUPS):
            at = (head * GROUPS + group) * HEAD_DIM
            query = turn(queries[at : at + HEAD_DIM], cosine, sine_table) * scale
            query_ref[head, :, group * rows : (group + 1) * rows] = query.astype(jnp.bfloat16)
    nothing = jnp.zeros((HEAD_DIM, rows), jnp.bfloat16)
    for head in range(KV_HEADS):
        for group in range(GROUPS):
            piece = slice(group * rows, (group + 1) * rows)
            query_pad[head, piece, :] = jnp.concatenate(
                [query_ref[head, :, piece], nothing], axis=0
            ).T
    weights[7].wait()
    turned_cotangent[...] = cotangent_ref[...].T
    acc[...] = jnp.zeros_like(acc)
    top[...] = jnp.full_like(top, MASKED)
    id_row = jnp.concatenate([id_ref[...].astype(jnp.float32)] * GROUPS, axis=1)
    local = jnp.concatenate([lax.broadcasted_iota(jnp.int32, (1, rows), 1)] * GROUPS, axis=1)
    index = place * rows + local
    ones = jnp.ones((16, rows), jnp.bfloat16)

    def attend_block(chip, half, careful):
        begin = half * rows
        columns = pl.ds(pl.multiple_of(begin, 128), rows)
        first = first_ref[chip] - begin
        limit = index - chip * span - begin
        inside = first <= 0
        for head in range(KV_HEADS):
            key_at = ID_ROWS + 2 * HEAD_DIM * head
            key_t = kv[chip, pl.ds(key_at, HEAD_DIM), columns]
            value_t = kv[chip, pl.ds(key_at + HEAD_DIM, HEAD_DIM), columns]
            scores = transposed_times(key_t, query_ref[head])
            old = top[head]
            if careful:
                key_index = lax.broadcasted_iota(jnp.int32, scores.shape, 0)
                allowed = (key_index >= first) & (key_index <= limit)
                scores = jnp.where(allowed, scores, 2 * MASKED)
            new = jnp.maximum(old, jnp.max(scores, axis=0, keepdims=True))
            less = new
            if not careful:
                new = jnp.where(inside, new, old)
                less = jnp.where(inside, new, -MASKED)
            probs = jnp.exp2(scores - less).astype(jnp.bfloat16)
            acc[head] = acc[head] * jnp.exp2(old - new) + matmul(
                jnp.concatenate([value_t, ones], axis=0), probs
            )
            top[head] = new

    def one_block(turn_number, carry):
        chip, mates = level - lax.div(turn_number, 2), lax.rem(turn_number, 2)
        half = core + mates * (1 - 2 * core)
        block = 2 * chip + half

        @pl.when(chip >= 0)
        def _():
            for head in range(KV_HEADS):
                @pl.when((mates == 0) & (chip < level))
                def _(head=head):
                    upward(chip, head).wait_recv()
                    hand_on(chip, head)

                @pl.when(mates == 1)
                def _(head=head):
                    across(chip, head).wait_recv()

            @pl.when(mates == 1)
            def _():
                first_ref[chip] = first_allowed(kv, chip, id_row)

            @pl.when(mates == 0)
            def _():
                first_ref[chip] = first_in_half(kv, chip, own, id_row) + half * rows

            edge = (block == 0) | (block == place)

            @pl.when((block <= place) & edge)
            def _():
                attend_block(chip, half, True)

            @pl.when((block < place) & jnp.logical_not(edge))
            def _():
                attend_block(chip, half, False)

        return carry

    lax.fori_loop(0, 2 * levels, one_block, 0)
    for head in range(KV_HEADS):
        total = acc[head, HEAD_DIM : HEAD_DIM + 1, :]
        result = acc[head, :HEAD_DIM, :] * (1.0 / total)
        attended[head] = result
        top[head] = top[head] + jnp.log2(total)
        for group in range(GROUPS):
            at = (head * GROUPS + group) * HEAD_DIM
            piece = result[:, group * rows : (group + 1) * rows]
            mixed_t[pl.ds(at, HEAD_DIM), :] = piece.astype(jnp.bfloat16)

    for copy in weights[3:7]:
        copy.wait()
    residual = x_ref[...].astype(jnp.float32) + transposed_times(out_w[...], mixed_t[...])
    mean = jnp.sum(residual * residual, axis=0, keepdims=True) * (1.0 / features)
    inverse_ffn = lax.rsqrt(mean + NORM_EPS)
    ffn_gain = as_column(ffn_gain_ref[...].reshape(1, features))
    normed_ffn_t = (residual * inverse_ffn * ffn_gain).astype(jnp.bfloat16)
    normed_ffn = normed_ffn_t.T
    cotangent_t = cotangent_ref[...]
    cotangent = turned_cotangent[...]
    residual_t[...] = residual
    unit_t[...] = residual * inverse_ffn
    normed_grad[...] = jnp.zeros_like(normed_grad)
    for number, at in enumerate(range(0, wide, FF_CHUNK)):
        piece = slice(at, at + FF_CHUNK)
        gate = matmul(normed_ffn, gate_w[:, piece])
        up = matmul(normed_ffn, up_w[:, piece])
        sigmoid = 1.0 / (1.0 + jnp.exp(-gate))
        silu = gate * sigmoid
        hidden = (silu * up).astype(jnp.bfloat16)
        down_part[:, piece] = matmul(cotangent_t, hidden).astype(jnp.bfloat16)
        streams[3 * number].run(0, carries)
        grad_hidden = matmul(cotangent, down_w[:, piece])
        gate_grad = (grad_hidden * up * sigmoid * (1.0 + gate * (1.0 - sigmoid))).astype(
            jnp.bfloat16
        )
        up_grad = (grad_hidden * silu).astype(jnp.bfloat16)
        gate_part[:, piece] = matmul(normed_ffn_t, gate_grad).astype(jnp.bfloat16)
        streams[3 * number + 1].run(0, carries)
        up_part[:, piece] = matmul(normed_ffn_t, up_grad).astype(jnp.bfloat16)
        streams[3 * number + 2].run(0, carries)
        residual_t[...] += times_transposed(down_w[:, piece], hidden)
        normed_grad[...] += times_transposed(gate_w[:, piece], gate_grad) + times_transposed(
            up_w[:, piece], up_grad
        )
        pump(number)
    layer_out[...] = residual_t[...].astype(jnp.bfloat16)
    unit = unit_t[...]
    grad_normed = normed_grad[...]
    gain_grad = jnp.sum(grad_normed * unit, axis=1, keepdims=True)
    inner = grad_normed * ffn_gain
    mean = jnp.sum(inner * unit, axis=0, keepdims=True) * (1.0 / features)
    branch = cotangent_t.astype(jnp.float32) + inverse_ffn * (inner - unit * mean)
    residual_t[...] = branch
    branch = branch.astype(jnp.bfloat16)
    out_grads = times_transposed(mixed_t[...], branch)
    fill = jnp.broadcast_to(gain_grad, (features, out_part.shape[0] - features)).T
    out_part[:features, :] = out_grads.astype(jnp.bfloat16)
    out_part[features:, :] = fill.astype(jnp.bfloat16)
    chunks = wide // FF_CHUNK
    streams[3 * chunks].run(0, carries)
    mixed_grad = matmul(out_w[...], branch).astype(jnp.bfloat16)
    for head in range(KV_HEADS):
        for group in range(GROUPS):
            at = (head * GROUPS + group) * HEAD_DIM
            piece = slice(group * rows, (group + 1) * rows)
            grad = mixed_grad[at : at + HEAD_DIM, :]
            grad_ref[head, :, piece] = grad
            delta_ref[head, :, piece] = jnp.sum(
                grad.astype(jnp.float32) * attended[head, :, piece], axis=0, keepdims=True
            )
            grad_pad[head, piece, :] = jnp.concatenate([nothing, grad], axis=0).T
    pump(chunks)
    back[...] = jnp.zeros_like(back)

    def attend_back(step, half, careful):
        head = lax.div(step, levels)
        chip = lax.rem(step, levels)
        key_at = pl.multiple_of(ID_ROWS + 2 * HEAD_DIM * head, 16)
        value_at = pl.multiple_of(ID_ROWS + 2 * HEAD_DIM * head + HEAD_DIM, 16)
        begin = half * rows
        first = first_ref[chip] - begin
        limit = index - chip * span - begin
        less = top[head]
        if not careful:
            less = jnp.where(first <= 0, less, -MASKED)
        for at in range(0, rows, BACK_CHUNK):
            size = min(BACK_CHUNK, rows - at)
            columns = pl.ds(pl.multiple_of(begin + at, 128), size)
            key_t = kv[chip, pl.ds(key_at, HEAD_DIM), columns]
            value_t = kv[chip, pl.ds(value_at, HEAD_DIM), columns]
            scores = transposed_times(key_t, query_ref[head])
            if careful:
                key_index = at + lax.broadcasted_iota(jnp.int32, scores.shape, 0)
                allowed = (key_index >= first) & (key_index <= limit)
                scores = jnp.where(allowed, scores, MASKED)
            probs = jnp.exp2(scores - less)
            prob_grad = transposed_times(value_t, grad_ref[head])
            score_grad = (probs * (prob_grad - delta_ref[head])).astype(jnp.bfloat16)
            kv_back = matmul(score_grad, query_pad[head]) + matmul(
                probs.astype(jnp.bfloat16), grad_pad[head]
            )
            part[step, pl.ds(pl.multiple_of(begin + at, 128), size), :] = kv_back.astype(
                jnp.bfloat16
            )
            back[head] += matmul(key_t, score_grad)

    mate_rows = pl.ds(pl.multiple_of((1 - core) * rows, 128), rows)

    def to_mate(step):
        return pltpu.make_async_remote_copy(
            src_ref=part.at[step, mate_rows], dst_ref=from_mate.at[step],
            send_sem=mate_send.at[step], recv_sem=mate_recv.at[step],
            device_id=mate, device_id_type=MESH,
        )

    def to_below(step):
        return pltpu.make_async_remote_copy(
            src_ref=part.at[step, own], dst_ref=from_above.at[step],
            send_sem=down_send.at[step], recv_sem=above_recv.at[step],
            device_id=below, device_id_type=MESH,
        )

    def collect(step):
        chip = lax.rem(step, levels)
        to_mate(step).wait_recv()
        both = part[step, own, :].astype(jnp.float32) + from_mate[step].astype(jnp.float32)
        part[step, own, :] = both.astype(jnp.bfloat16)

        @pl.when(level < levels - 1)
        def _():
            to_below(step).wait_recv()
            more = part[step, own, :].astype(jnp.float32) + from_above[step].astype(jnp.float32)
            part[step, own, :] = more.astype(jnp.bfloat16)

        @pl.when(chip < level)
        def _():
            to_below(step).start()

    base = (place * rows).astype(jnp.float32) * inverse_in[...]
    base_cosine, base_sine = jnp.cos(base), -jnp.sin(base)
    back_cosine[...] = base_cosine * cosine_in[...] + base_sine * sine_in[...]
    back_sine[...] = base_sine * cosine_in[...] - base_cosine * sine_in[...]

    def head_done(head):
        cosine, sine_table = back_cosine[...], back_sine[...]
        step = head * levels + level
        both = part[step, own, :].astype(jnp.float32).T
        key_back = turn(both[:HEAD_DIM] * LN2, cosine, sine_table).astype(jnp.bfloat16)
        value_back = both[HEAD_DIM:].astype(jnp.bfloat16)
        kv_back = jnp.concatenate([key_back, value_back], axis=0)
        at = pl.multiple_of(head * 2 * HEAD_DIM, 2 * HEAD_DIM)
        turned_kv[pl.ds(at, 2 * HEAD_DIM), :] = kv_back
        kv_part[pl.ds(at, 2 * HEAD_DIM), :] = times_transposed(kv_back, normed_t[...]).astype(
            jnp.bfloat16
        )
        query_back = jnp.concatenate(
            [
                turn(
                    back[head, :, group * rows : (group + 1) * rows] * (1.0 / math.sqrt(HEAD_DIM)),
                    cosine, sine_table,
                ).astype(jnp.bfloat16)
                for group in range(GROUPS)
            ],
            axis=0,
        )
        wide_at = pl.multiple_of(head * GROUPS * HEAD_DIM, HEAD_DIM)
        turned_query[pl.ds(wide_at, GROUPS * HEAD_DIM), :] = query_back
        spare = jnp.zeros((features, QUERY_COLUMNS - GROUPS * HEAD_DIM), jnp.float32)
        query_part[pl.ds(pl.multiple_of(head * features, features), features), :] = jnp.concatenate(
            [times_transposed(normed_t[...], query_back), spare], axis=1
        ).astype(jnp.bfloat16)

    def one_step(turn_number, carry):
        step, own_turn = lax.div(turn_number, 2), lax.rem(turn_number, 2)
        half = core + (1 - own_turn) * (1 - 2 * core)
        chip = lax.rem(step, levels)
        block = 2 * chip + half

        @pl.when((step < count) & (chip <= level))
        def _():
            edge = (block == 0) | (block == place)

            @pl.when((block <= place) & edge)
            def _():
                attend_back(step, half, True)

            @pl.when((block < place) & jnp.logical_not(edge))
            def _():
                attend_back(step, half, False)

            @pl.when(block > place)
            def _():
                part[step, mate_rows, :] = jnp.zeros((rows, 2 * HEAD_DIM), jnp.bfloat16)

            @pl.when(own_turn == 0)
            def _():
                to_mate(step).start()

        due = step - levels + level

        @pl.when((own_turn == 1) & (due >= 0) & (due < count))
        def _():
            @pl.when(lax.rem(due, levels) <= level)
            def _():
                collect(due)

        ended = lax.div(step, levels) - 1

        @pl.when((own_turn == 1) & (step > 0) & (lax.rem(step, levels) == 0))
        def _():
            head_done(ended)
            for head in range(KV_HEADS):
                @pl.when(ended == head)
                def _(head=head):
                    streams[3 * chunks + 1 + 2 * head].run(0, carries)
                    streams[3 * chunks + 2 + 2 * head].run(0, carries)

        for begin in range(0, 2 * (count + 1), SLOTS):
            some = range(begin, begin + SLOTS)

            @pl.when((turn_number >= begin) & (turn_number < begin + SLOTS))
            def _(some=some):
                for number in some:
                    if number + chunks + 1 in pumps:
                        @pl.when(turn_number == number)
                        def _(slot=number + chunks + 1):
                            pump(slot)

        return carry

    lax.fori_loop(0, 2 * (count + 1), one_step, 0)

    grad_t = matmul(query_w[...], turned_query[...])
    for head in range(KV_HEADS):
        at = head * HEAD_DIM
        weight = jnp.concatenate(
            [key_w[at : at + HEAD_DIM, :], value_w[at : at + HEAD_DIM, :]], axis=0
        )
        grad_t += transposed_times(weight, turned_kv[2 * at : 2 * at + 2 * HEAD_DIM, :])
    x = x_ref[...].astype(jnp.float32)
    mean = jnp.sum(x * x, axis=0, keepdims=True) * (1.0 / features)
    inverse_attn = lax.rsqrt(mean + NORM_EPS)
    unit = x * inverse_attn
    gain_column = jnp.sum(grad_t * unit, axis=1, keepdims=True)
    gain_rows = jnp.broadcast_to(gain_column, (features, 128)).T
    gain_part[...] = gain_rows[: gain_part.shape[0]].astype(jnp.bfloat16)
    streams[-1].run(0, carries)
    first_ops = len(after) // 3
    for number, op in after[:first_ops]:
        streams[number].run(op, carries)
    inner = grad_t * as_column(attn_gain_ref[...].reshape(1, features))
    mean = jnp.sum(inner * unit, axis=0, keepdims=True) * (1.0 / features)
    input_grad[...] = (residual_t[...] + inverse_attn * (inner - unit * mean)).astype(jnp.bfloat16)
    for number, op in after[first_ops:]:
        streams[number].run(op, carries)
    for stream in streams:
        stream.drain(carries)

    def ended(step, carry):
        chip = lax.rem(step, levels)

        @pl.when(chip <= level)
        def _():
            to_mate(step).wait_send()

        @pl.when(chip < level)
        def _():
            to_below(step).wait_send()

        return carry

    lax.fori_loop(0, count, ended, 0)

    def handed_on(chip, carry):
        @pl.when(chip <= level)
        def _():
            for head in range(KV_HEADS):
                across(chip, head).wait_send()

                @pl.when(level < levels - 1)
                def _(head=head):
                    upward(chip, head).wait_send()

        return carry

    lax.fori_loop(0, levels, handed_on, 0)


def rotary_tables(rows):
    half_size = HEAD_DIM // 2
    inverse = (ROPE_BASE ** (-np.arange(half_size, dtype=np.float64) * 2.0 / HEAD_DIM))[:, None]
    phase = inverse * np.arange(rows, dtype=np.float64)[None, :]
    return tuple(
        jnp.asarray(table, jnp.float32) for table in (np.cos(phase), np.sin(phase), inverse)
    )


def layer(x_t, ids, attn_gain, ffn_gain, w_query, w_key_t, w_value_t, w_out, w_gate, w_up,
          w_down_t, cotangent_t):
    dp_count, ctx_count = lax.axis_size("dp"), lax.axis_size("ctx")
    order = plane_order(dp_count)
    crossed = crossed_order(order, ctx_count)
    level_bits = (ctx_count // 2).bit_length() - 1
    levels = ctx_count // 2
    features, rows = x_t.shape
    wide = w_gate.shape[1]
    span, queries = 2 * rows, GROUPS * rows
    count = KV_HEADS * levels
    chunks = wide // FF_CHUNK

    jobs = [(True, "rrc", (features, FF_CHUNK))] * (3 * chunks)
    jobs += [(True, "rrr", (OUT_ROWS, features))]
    for head in range(KV_HEADS):
        folded = head < KV_HEADS - 1
        jobs += [(folded, "rrc", (features, QUERY_COLUMNS)), (folded, "rrr", (2 * HEAD_DIM, features))]
    jobs += [(False, "", (16, features))]
    slots = [FEED_US * number for number in range(chunks)]
    slots.append(slots[-1] + OUT_US)
    turns = 2 * (count + 1)
    slots += [slots[-1] + STEP_US * (number + 1) for number in range(turns)]
    slots.append(slots[-1] + TAIL_US)
    begins = [number // 3 for number in range(3 * chunks)] + [chunks]
    for head in range(KV_HEADS):
        begins += [chunks + 2 * (head + 1) * levels + 2] * 2
    begins += [len(slots) - 1]
    relayed = [
        chunks + 2 + 2 * step for step in range(count) if step % levels < levels - 1
    ]
    pumps, after = {}, []
    for slot, number, op in planned(
        [
            (
                len(order), 0 if folded else level_bits, level_bits, cuts, 2 * shape[0] * shape[1],
                begin,
            )
            for (folded, cuts, shape), begin in zip(jobs, begins)
        ],
        slots, relayed,
    ):
        if op == 0:
            continue
        if slot <= chunks + turns:
            pumps.setdefault(slot, []).append((number, op))
        else:
            after.append((number, op))

    vmem = lambda shape, dtype=jnp.bfloat16: pltpu.VMEM(shape, dtype)
    lands = [
        [
            vmem(size)
            for size in (
                landing_shapes(*shape, cuts, len(order), level_bits)
                if folded
                else landing_shapes(*shape, cuts, len(crossed), 0)
            )
        ]
        for folded, cuts, shape in jobs
    ]
    dma = lambda *shape: pltpu.SemaphoreType.DMA(shape)
    semaphores = len(order) + level_bits + HALVINGS + 2
    head_t = (KV_HEADS, HEAD_DIM, queries)
    padded = (KV_HEADS, queries, 2 * HEAD_DIM)
    row = (KV_HEADS, 1, queries)
    f32 = jnp.float32
    totals = [(features, wide)] * 3 + [(OUT_ROWS, features)]
    totals += [(KV_HEADS * features, QUERY_COLUMNS), (2 * KV_HEADS * HEAD_DIM, features)]
    totals += [(16, features)]
    anywhere = pl.BlockSpec(memory_space=pl.ANY)
    return pl.pallas_call(
        functools.partial(layer_kernel, order, crossed, level_bits, jobs, pumps, after),
        out_shape=tuple(
            jax.ShapeDtypeStruct(shape, jnp.bfloat16) for shape in [(features, rows)] * 2 + totals
        ),
        in_specs=in_vmem(7) + [anywhere] * 8,
        out_specs=tuple(in_vmem(2) + [anywhere] * 7),
        scratch_shapes=[
            vmem(w_query.shape), vmem(w_key_t.shape), vmem(w_value_t.shape), vmem(w_out.shape),
            vmem(w_gate.shape), vmem(w_up.shape), vmem(w_down_t.shape), vmem((features, rows)),
            vmem((levels, ID_ROWS + 2 * KV_HEADS * HEAD_DIM, span)),
            vmem(head_t), vmem(padded), vmem(head_t), vmem(padded),
            vmem((levels, 1, queries), jnp.int32),
            vmem((features, rows)),
            vmem(head_t, f32),
            vmem((KV_HEADS, HEAD_DIM + 16, queries), f32),
            vmem(row, f32), vmem(row, f32),
            vmem((features, rows)),
            *[vmem((features, rows), f32) for _ in range(3)],
            vmem(head_t, f32),
            vmem((count, span, 2 * HEAD_DIM)),
            vmem((count, rows, 2 * HEAD_DIM)), vmem((count, rows, 2 * HEAD_DIM)),
            vmem((2 * KV_HEADS * HEAD_DIM, rows)), vmem((HEADS * HEAD_DIM, rows)),
            vmem((HEAD_DIM // 2, rows), f32), vmem((HEAD_DIM // 2, rows), f32),
            vmem((rows, features)),
            *[vmem(shape) for shape in totals],
            lands,
            dma(8),
            *[dma(levels, KV_HEADS) for _ in range(4)],
            *[dma(count) for _ in range(4)],
            dma(len(jobs), semaphores), dma(len(jobs), semaphores),
        ],
        compiler_params=pltpu.CompilerParams(
            collective_id=1, has_side_effects=True, vmem_limit_bytes=60 * 1024 * 1024
        ),
        name="layer",
    )(
        x_t, ids, attn_gain, ffn_gain, *rotary_tables(rows), w_query, w_key_t, w_value_t, w_out,
        w_gate, w_up, w_down_t, cotangent_t,
    )


PIECES = 2
SOME_ROWS = 48


def finish_kernel(
    layer_in, input_in, gate, up, down_t, out, query, kv, gain,
    layer_out, input_out, gate_out, up_out, down_out, out_out, key_out, value_out, query_out,
    gain_ffn, gain_attn,
    held, made, out_held, out_made, query_held, query_made, kv_held, key_made, value_made, passed,
    come, go,
):
    features = gate.shape[0]
    piece = features // PIECES
    passed_in = [
        pltpu.make_async_copy(source, passed.at[number], come.at[3 * PIECES + 3 + number])
        for number, source in enumerate((layer_in, input_in))
    ]
    passed_out = [
        pltpu.make_async_copy(passed.at[number], target, go.at[number])
        for number, target in enumerate((layer_out, input_out))
    ]
    wide = []
    for source, target in ((gate, gate_out), (up, up_out), (down_t, down_out)):
        for number in range(PIECES):
            rows, at = pl.ds(number * piece, piece), len(wide)
            wide.append(
                (
                    pltpu.make_async_copy(source.at[rows], held.at[at], come.at[at]),
                    pltpu.make_async_copy(made.at[at], target.at[rows], go.at[2 + at]),
                )
            )
    at = len(wide)
    small_in = [
        pltpu.make_async_copy(source, target, come.at[at + number])
        for number, (source, target) in enumerate(
            ((out, out_held), (query, query_held), (kv, kv_held))
        )
    ]
    small_out = [
        pltpu.make_async_copy(source, target, go.at[2 + at + number])
        for number, (source, target) in enumerate(
            (
                (out_made, out_out), (query_made, query_out), (key_made, key_out),
                (value_made, value_out),
            )
        )
    ]
    for arrival, _ in wide:
        arrival.start()
    for copy in small_in + passed_in:
        copy.start()

    def by_rows(count, convert):
        def some(step, carry):
            convert(pl.ds(pl.multiple_of(step * SOME_ROWS, 16), SOME_ROWS), step * SOME_ROWS)
            return carry

        lax.fori_loop(0, count // SOME_ROWS, some, 0)

    for at, (arrival, departure) in enumerate(wide):
        arrival.wait()

        def convert(rows, start, at=at):
            made[at, rows, :] = held[at, rows, :].astype(jnp.float32)

        by_rows(piece, convert)
        departure.start()

    small_in[0].wait()

    def convert_out(rows, start):
        out_made[rows, :] = out_held[rows, :].astype(jnp.float32)

    by_rows(features, convert_out)
    small_out[0].start()
    gain_ffn[...] = out_held[OUT_ROWS - 16 :, :].astype(jnp.float32)[-1]
    small_in[1].wait()
    width = GROUPS * HEAD_DIM

    def convert_query(rows, start):
        query_made[rows, :] = jnp.concatenate(
            [
                query_held[
                    pl.ds(pl.multiple_of(head * features + start, 16), SOME_ROWS), :
                ].astype(jnp.float32)[:, :width]
                for head in range(KV_HEADS)
            ],
            axis=1,
        )

    by_rows(features, convert_query)
    small_out[1].start()
    gain_attn[...] = gain[...].astype(jnp.float32)[-1]
    small_in[2].wait()
    for head in range(KV_HEADS):
        at = head * HEAD_DIM
        key_made[at : at + HEAD_DIM, :] = kv_held[2 * at : 2 * at + HEAD_DIM, :].astype(jnp.float32)
        value_made[at : at + HEAD_DIM, :] = kv_held[
            2 * at + HEAD_DIM : 2 * at + 2 * HEAD_DIM, :
        ].astype(jnp.float32)
    small_out[2].start()
    small_out[3].start()
    for arrival, departure in zip(passed_in, passed_out):
        arrival.wait()
        departure.start()
    for copy in passed_out + [departure for _, departure in wide] + small_out:
        copy.wait()


def finish(layer_t, input_t, down_t, gate, up, out, query, kv, gain):
    features, wide = gate.shape
    key_width = KV_HEADS * HEAD_DIM
    f32 = jnp.float32
    anywhere = pl.BlockSpec(memory_space=pl.ANY)
    shape = lambda *dims: jax.ShapeDtypeStruct(dims, f32)
    short = jax.ShapeDtypeStruct(layer_t.shape, layer_t.dtype)
    vmem = lambda *dims: pltpu.VMEM(dims, jnp.bfloat16)
    vmem_f32 = lambda *dims: pltpu.VMEM(dims, f32)
    copies = 3 * PIECES
    return pl.pallas_call(
        finish_kernel,
        out_shape=(
            short, short,
            shape(features, wide), shape(features, wide), shape(features, wide),
            shape(features, features), shape(key_width, features), shape(key_width, features),
            shape(features, features), shape(features), shape(features),
        ),
        in_specs=[anywhere] * 8 + in_vmem(1),
        out_specs=tuple([anywhere] * 9 + in_vmem(2)),
        scratch_shapes=[
            vmem(copies, features // PIECES, wide), vmem_f32(copies, features // PIECES, wide),
            vmem(OUT_ROWS, features), vmem_f32(features, features),
            vmem(*query.shape), vmem_f32(features, features),
            vmem(*kv.shape), vmem_f32(key_width, features), vmem_f32(key_width, features),
            vmem(2, *layer_t.shape),
            pltpu.SemaphoreType.DMA((copies + 5,)), pltpu.SemaphoreType.DMA((copies + 6,)),
        ],
        compiler_params=pltpu.CompilerParams(vmem_limit_bytes=60 * 1024 * 1024),
        name="finish",
    )(layer_t, input_t, gate, up, down_t, out, query, kv, gain)


def in_vmem(count):
    return [pl.BlockSpec(memory_space=pltpu.VMEM)] * count


def on_device(
    hidden_in, segment_ids, w_query, w_key, w_value, w_out, w_gate, w_up, w_down, gain_attn,
    gain_ffn, out_grad,
):
    summed = layer(
        hidden_in[0].T, segment_ids, gain_attn, gain_ffn, w_query, w_key.T, w_value.T,
        w_out, w_gate, w_up, w_down.T, out_grad[0].T,
    )
    (
        layer_t, input_t, grad_gate, grad_up, grad_down_t, grad_out, grad_key_t, grad_value_t,
        grad_query, grad_gain_ffn, grad_gain_attn,
    ) = finish(*summed)
    return (
        layer_t.T[None], input_t.T[None], grad_query, grad_key_t.T, grad_value_t.T, grad_out,
        grad_gate, grad_up, grad_down_t.T, grad_gain_attn, grad_gain_ffn,
    )


def solution(mesh):
    rows = P("dp", "ctx", None)
    return jax.shard_map(
        on_device,
        mesh=mesh,
        in_specs=(rows, P("dp", "ctx")) + (P(),) * 9 + (rows,),
        out_specs=(rows, rows) + (P(),) * 9,
        check_vma=False,
    )
```

```python
import functools
import math

import jax
import jax.numpy as jnp
import numpy as np
from jax import lax
from jax.experimental import pallas as pl
from jax.experimental.pallas import tpu as pltpu
from jax.sharding import PartitionSpec as P

HEADS = 9
KV_HEADS = 3
HEAD_DIM = 64
GROUPS = HEADS // KV_HEADS

NORM_EPS = 1e-05
ROPE_BASE = 10000.0
MASKED = -1e30
LOG2E = 1.4426950408889634
LN2 = 0.6931471805599453
MESH = pl.DeviceIdType.MESH
OUT_ROWS = 640
QUERY_COLUMNS = 256
ID_ROWS = 16
CHUNK = 256
FF_CHUNK = 512
BACK_CHUNK = 384


def matmul(left_side, right_side):
    return jnp.dot(left_side, right_side, preferred_element_type=jnp.float32)


def times_transposed(left_side, right_side):
    return lax.dot_general(
        left_side, right_side, (((1,), (1,)), ((), ())), preferred_element_type=jnp.float32
    )


def transposed_times(left_side, right_side):
    return lax.dot_general(
        left_side, right_side, (((0,), (0,)), ((), ())), preferred_element_type=jnp.float32
    )


def bit_of(place, bit):
    return lax.rem(lax.div(place, bit), 2)


def plane_order(dp_count):
    bits = [1 << i for i in range(dp_count.bit_length() - 1)]
    return [("ctx", 1, 1)] + [("dp", bit, bits[(i + 1) % len(bits)]) for i, bit in enumerate(bits)]


def sum_links(order, level_bits, slice_place, place):
    core, level = lax.rem(place, 2), lax.div(place, 2)
    picks, devices = [], []
    for axis, first, second in order:
        at = slice_place if axis == "dp" else place
        pick, bit = bit_of(at, first), first
        if second != first:
            pick = jnp.where(core == 0, pick, bit_of(at, second))
            bit = jnp.where(core == 0, first, second)
        partner = at + (1 - 2 * pick) * bit
        picks.append(pick)
        devices.append((partner, place) if axis == "dp" else (slice_place, partner))
    mirrors = []
    for number in range(level_bits):
        size = 2 << number
        group = lax.div(level, size) * size
        mirrors.append((slice_place, 2 * (2 * group + size - 1 - level) + core))
    return picks, devices, mirrors


def crossed_order(order, ctx_count):
    bits = [1 << i for i in range(1, ctx_count.bit_length() - 1)]
    return order + [("ctx", bit, bits[(i + 1) % len(bits)]) for i, bit in enumerate(bits)]


def is_inner(level):
    return lax.rem(level, 2) != lax.rem(lax.div(level, 2), 2)


HALVINGS = 3
SLOTS = 5


def halved_shapes(rows, columns, cuts):
    shapes = []
    for cut in cuts:
        rows, columns = (rows // 2, columns) if cut == "r" else (rows, columns // 2)
        shapes.append((rows, columns))
    return shapes


def landing_shapes(rows, columns, cuts, plane, level_bits):
    shapes = halved_shapes(rows, columns, cuts)
    last = shapes[-1] if shapes else (rows, columns)
    return shapes + [last] * (plane - len(cuts) + (level_bits + 1 if level_bits else 0))


class Summed:
    def __init__(self, links, level_bits, cuts, source, corner, shape, landed, total, send, recv):
        self.picks, self.devices, self.mirrors = links
        self.level_bits, self.cuts = level_bits, cuts
        self.landed, self.total = landed, total
        self.source, self.corner, self.shape = source, corner, shape
        self.send, self.recv = send, recv
        self.plane = len(self.picks)
        self.count = self.plane + (level_bits + 1 if level_bits else 0)
        self.final = landed[-1]

    def cut_at(self, corner, shape, cut, pick):
        rows, columns = shape
        row, column = corner
        if cut == "r":
            rows //= 2
            row = row + pick * rows
        else:
            columns //= 2
            column = column + pick * columns
        return (row, column), (rows, columns)

    @staticmethod
    def view(ref, corner, shape):
        row, column = corner
        if not isinstance(row, int):
            row = pl.multiple_of(row, 16)
        if not isinstance(column, int):
            column = pl.multiple_of(column, 128)
        return ref.at[pl.ds(row, shape[0]), pl.ds(column, shape[1])]

    def current(self, stage):
        if stage == 0:
            return self.source, self.corner, self.shape
        return self.landed[stage - 1], (0, 0), self.landed[stage - 1].shape

    def copy(self, source, target, number, device):
        return pltpu.make_async_remote_copy(
            src_ref=source, dst_ref=target, send_sem=self.send.at[number],
            recv_sem=self.recv.at[number], device_id=device, device_id_type=MESH,
        )

    def outgoing(self, stage):
        ref, corner, shape = self.current(stage)
        if stage < self.plane:
            device = self.devices[stage]
            if stage < len(self.cuts):
                corner, shape = self.cut_at(corner, shape, self.cuts[stage], 1 - self.picks[stage])
        elif stage == self.plane or stage == self.count - 1:
            device = self.mirrors[0]
        else:
            device = self.mirrors[stage - self.plane]
        given = self.level_bits and stage == self.count - 1
        source = self.final if given else self.view(ref, corner, shape)
        return self.copy(source, self.landed[stage], stage, device)

    def add(self, stage, target=None):
        ref, corner, shape = self.current(stage)
        if stage < len(self.cuts):
            corner, shape = self.cut_at(corner, shape, self.cuts[stage], self.picks[stage])
        landed = self.landed[stage]
        target = landed if target is None else target
        row, column = corner
        if not isinstance(column, int):
            column = pl.multiple_of(column, 128)
        take = next(rows for rows in (80, 48, 64, 32, 16) if shape[0] % rows == 0)

        def some(step, carry):
            at = step * take
            near = ref[pl.ds(pl.multiple_of(row + at, 16), take), pl.ds(column, shape[1])]
            here = pl.ds(pl.multiple_of(at, 16), take)
            both = near.astype(jnp.float32) + landed[here, :].astype(jnp.float32)
            target[here, :] = both.astype(jnp.bfloat16)
            return carry

        lax.fori_loop(0, shape[0] // take, some, 0)

    def share(self, depth):
        corner, shape = (0, 0), self.shape
        for stage in range(depth):
            corner, shape = self.cut_at(corner, shape, self.cuts[stage], self.picks[stage])
        return self.view(self.total, (corner[0] + self.corner[0], corner[1] + self.corner[1]), shape)

    def settle(self):
        return pltpu.make_async_copy(
            self.final, self.share(len(self.cuts)), self.send.at[self.count + len(self.cuts)]
        )

    def handing(self, back):
        stage = len(self.cuts) - 1 - back
        mine = self.share(stage + 1)
        return self.copy(
            self.final if back == 0 else mine, mine, self.count + back, self.devices[stage]
        )

    def run(self, op, inner):
        if op == 0:
            self.outgoing(0).start()
        elif op <= self.plane:
            self.outgoing(op - 1).wait_recv()
            self.add(op - 1)
            if op < self.plane:
                self.outgoing(op).start()
            elif not self.level_bits:
                self.settle().start()
                if self.cuts:
                    self.handing(0).start()
                else:
                    self.settle().wait()
            else:
                @pl.when(jnp.logical_not(inner))
                def _():
                    self.outgoing(op).start()
        elif op < self.count:
            @pl.when(inner)
            def _():
                self.outgoing(op - 1).wait_recv()
                if op < self.count - 1:
                    self.add(op - 1)
                else:
                    self.add(op - 1, self.final)
                self.outgoing(op).start()
                if op == self.count - 1:
                    self.handing(0).start()
                    self.settle().start()
        elif op == self.count:
            @pl.when(jnp.logical_not(inner))
            def _():
                self.outgoing(op - 1).wait_recv()
                self.handing(0).start()
                self.settle().start()
        else:
            back = op - self.count - 1
            self.handing(back).wait_recv()
            if back == 0:
                self.settle().wait()
            if back + 1 < len(self.cuts):
                self.handing(back + 1).start()

    def drain(self, inner):
        for stage in range(self.plane):
            self.outgoing(stage).wait_send()

        if self.level_bits:
            @pl.when(inner)
            def _():
                for stage in range(self.plane + 1, self.count):
                    self.outgoing(stage).wait_send()

            @pl.when(jnp.logical_not(inner))
            def _():
                self.outgoing(self.plane).wait_send()

        for back in range(len(self.cuts)):
            self.handing(back).wait_send()


RATES = {"core": 250e3, "dp": 85e3, "ctx": 42e3}
HOP_US = 2.0
STEP_US = 1.15
FEED_US = 3.0
OUT_US = 3.0
TAIL_US = 2.0


def planned(jobs, slots, relayed):
    work = []
    for plane, crossed, level_bits, cuts, size, _ in jobs:
        sizes = []
        for stage in range(plane):
            size = size / 2 if stage < len(cuts) else size
            sizes.append(("dp" if stage else "core", size))
        levels = [("ctx", size)] * (crossed if crossed else level_bits + 1)
        levels = [(name + str(number), size) for number, (name, size) in enumerate(levels)]
        work.append(sizes + levels + sizes[: len(cuts)][::-1])
    free, arrival, done, plan = {}, {}, [0] * len(jobs), []

    def issue(number, now):
        stage = done[number]
        if stage < len(work[number]):
            link, size = work[number][stage]
            free[link] = max(now, free.get(link, 0.0)) + size / RATES[link.rstrip("0123456789")]
            arrival[number] = free[link] + HOP_US
        done[number] += 1

    def live():
        return [n for n in range(len(jobs)) if 0 < done[n] <= len(work[n])]

    now = 0.0
    for slot, end in enumerate(slots):
        now = max(now, end)
        if slot in relayed:
            for link in ("ctx0", "ctx1"):
                free[link] = max(free.get(link, 0.0), now) + 2.2
        for number, job in enumerate(jobs):
            if job[5] == slot:
                plan.append((slot, number, 0))
                issue(number, now)
        for number in sorted((n for n in live() if arrival[n] <= now), key=lambda n: -done[n]):
            plan.append((slot, number, done[number]))
            now += 0.2
            issue(number, now)
    while live():
        number = min(live(), key=lambda n: (max(arrival[n] - now, 0.0), -done[n]))
        now = max(now, arrival[number]) + 0.2
        plan.append((len(slots), number, done[number]))
        issue(number, now)
    return plan


def greet(certain, perhaps):
    barrier = pltpu.get_barrier_semaphore()
    for target in certain:
        pl.semaphore_signal(barrier, inc=1, device_id=target, device_id_type=MESH)
    for target, there in perhaps:
        @pl.when(there)
        def _(target=target):
            pl.semaphore_signal(barrier, inc=1, device_id=target, device_id_type=MESH)


def await_peers(certain, perhaps):
    count = len(certain)
    for _, there in perhaps:
        count = count + there.astype(jnp.int32)
    pl.semaphore_wait(pltpu.get_barrier_semaphore(), count)


def before(ids, id_row):
    ids = ids[:1].astype(jnp.float32)
    first = jnp.zeros(id_row.shape, jnp.float32)
    for value in range(3):
        number = jnp.sum((ids == value).astype(jnp.float32), axis=1, keepdims=True)
        first += jnp.where(id_row > value, number, 0.0)
    return first.astype(jnp.int32)


def first_allowed(kv_ref, chip, id_row):
    return sum(before(kv_ref[chip, core, pl.ds(0, ID_ROWS), :], id_row) for core in (0, 1))


def first_in_half(kv_ref, chip, core, id_row):
    return before(kv_ref[chip, core, pl.ds(0, ID_ROWS), :], id_row)


def turn(values, cosine, sine_table):
    half_size = HEAD_DIM // 2
    first_half = values[:half_size]
    second_half = values[half_size:]
    return jnp.concatenate(
        [
            first_half * cosine - second_half * sine_table,
            second_half * cosine + first_half * sine_table,
        ],
        axis=0,
    )


def stack_halves(ref, at, values):
    rows, columns = values.shape
    values = values.astype(jnp.bfloat16)
    if not isinstance(at, int):
        at = pl.multiple_of(at, 16)
    ref[pl.ds(at, rows), :] = values[:, : columns // 2]
    ref[pl.ds(at + rows, rows), :] = values[:, columns // 2 :]


def with_lanes(values, lanes):
    fill = jnp.zeros((values.shape[0], lanes - values.shape[1]), values.dtype)
    return jnp.concatenate([values, fill], axis=1)


def as_column(row):
    return jnp.broadcast_to(row, (8, row.shape[1])).T[:, :1]


def layer_kernel(
    order, crossed, level_bits, jobs, pumps, after,
    x_ref, id_ref, attn_gain_ref, ffn_gain_ref, cosine_in, sine_in, inverse_in,
    query_hbm, key_hbm, value_hbm, out_hbm, gate_hbm, up_hbm, down_hbm, cotangent_hbm,
    layer_out, input_grad, down_total, gate_total, up_total, out_total, query_total,
    kv_total, gain_total,
    query_w, key_w, value_w, out_w, gate_w, up_w, down_w, cotangent_ref,
    kv, query_ref, query_pad, grad_ref, grad_pad, first_ref, normed_t, attended, acc, top,
    delta_ref, mixed_t, residual_t, unit_t, normed_grad, back, part, from_mate, from_above, turned_kv,
    turned_query, back_cosine, back_sine, turned_cotangent,
    down_part, gate_part, up_part, out_part, query_part, kv_part, gain_part, lands,
    loads, up_send, below_recv, over_send, over_recv, mate_send, mate_recv, down_send, above_recv,
    sum_send, sum_recv,
):
    place = lax.axis_index("ctx")
    core, level = lax.rem(place, 2), lax.div(place, 2)
    levels, _, _, rows = kv.shape
    span = 2 * rows
    features = x_ref.shape[0]
    wide = gate_w.shape[1]
    chunks = wide // FF_CHUNK
    count = KV_HEADS * levels
    slice_place = lax.axis_index("dp")
    mate = (slice_place, place + 1 - 2 * core)
    below = (slice_place, place - 2)
    above = (slice_place, place + 2)
    links = {
        True: sum_links(order, level_bits, slice_place, place),
        False: sum_links(crossed, 0, slice_place, place),
    }
    own = pl.ds(pl.multiple_of(core * rows, 128), rows)

    weights = [
        pltpu.make_async_copy(source, target, loads.at[number])
        for number, (source, target) in enumerate(
            (
                (key_hbm, key_w), (value_hbm, value_w), (query_hbm, query_w), (out_hbm, out_w),
                (gate_hbm, gate_w), (up_hbm, up_w), (down_hbm, down_w),
                (cotangent_hbm, cotangent_ref),
            )
        )
    ]
    for copy in weights:
        copy.start()

    carries = is_inner(level)
    side = 2 * bit_of(level, 1) - 1
    other = level + side
    certain = links[False][1]
    perhaps = [((slice_place, place + 2 * side), (other >= 0) & (other < levels))]
    perhaps += [(device, carries) for device in links[True][2][2:]]
    greet(certain, perhaps)

    sources = [(down_part, down_total), (gate_part, gate_total), (up_part, up_total)]
    places = [
        (*pair, (2 * features * number, 0)) for number in range(wide // FF_CHUNK) for pair in sources
    ]
    places += [(out_part, out_total, (0, 0))]
    for head in range(KV_HEADS):
        places += [
            (query_part, query_total, (2 * head * features, 0)),
            (kv_part, kv_total, (head * 2 * HEAD_DIM, 0)),
        ]
    places += [(gain_part, gain_total, (0, 0))]
    streams = [
        Summed(
            links[folded], level_bits if folded else 0, cuts, source, corner, shape, lands[number], total,
            sum_send.at[number], sum_recv.at[number],
        )
        for number, ((source, total, corner), (folded, cuts, shape)) in enumerate(zip(places, jobs))
    ]

    def pump(slot):
        for number, op in pumps.get(slot, ()):
            streams[number].run(op, carries)

    x = x_ref[...].astype(jnp.float32)
    mean = jnp.sum(x * x, axis=0, keepdims=True) * (1.0 / features)
    inverse_attn = lax.rsqrt(mean + NORM_EPS)
    attn_gain = as_column(attn_gain_ref[...].reshape(1, features))
    normed_t[...] = (x * inverse_attn * attn_gain).astype(jnp.bfloat16)
    base = (place * rows).astype(jnp.float32) * inverse_in[...]
    base_cosine, base_sine = jnp.cos(base), jnp.sin(base)
    cosine = base_cosine * cosine_in[...] - base_sine * sine_in[...]
    sine_table = base_sine * cosine_in[...] + base_cosine * sine_in[...]
    kv[level, core, pl.ds(0, ID_ROWS), :] = jnp.broadcast_to(
        id_ref[...].astype(jnp.float32), (ID_ROWS, rows)
    ).astype(jnp.bfloat16)
    weights[0].wait()
    weights[1].wait()

    def piece_rows(head):
        if head == 0:
            return pl.ds(0, ID_ROWS + 2 * HEAD_DIM)
        return pl.ds(ID_ROWS + 2 * HEAD_DIM * head, 2 * HEAD_DIM)

    def upward(chip, head):
        return pltpu.make_async_remote_copy(
            src_ref=kv.at[chip, core, piece_rows(head)], dst_ref=kv.at[chip, core, piece_rows(head)],
            send_sem=up_send.at[chip, head], recv_sem=below_recv.at[chip, head],
            device_id=above, device_id_type=MESH,
        )

    def across(chip, head):
        return pltpu.make_async_remote_copy(
            src_ref=kv.at[chip, core, piece_rows(head)], dst_ref=kv.at[chip, core, piece_rows(head)],
            send_sem=over_send.at[chip, head], recv_sem=over_recv.at[chip, head],
            device_id=mate, device_id_type=MESH,
        )

    def hand_on(chip, head):
        @pl.when(level < levels - 1)
        def _():
            upward(chip, head).start()

        across(chip, head).start()

    keys = matmul(key_w[...], normed_t[...])
    values = matmul(value_w[...], normed_t[...])
    await_peers(certain, perhaps)
    for head in range(KV_HEADS):
        at = head * HEAD_DIM
        key = turn(keys[at : at + HEAD_DIM], cosine, sine_table)
        both = jnp.concatenate([key, values[at : at + HEAD_DIM]], axis=0)
        kv[level, core, pl.ds(ID_ROWS + 2 * at, 2 * HEAD_DIM), :] = both.astype(jnp.bfloat16)
        hand_on(level, head)
    weights[2].wait()
    queries = transposed_times(query_w[...], normed_t[...])
    scale = LOG2E / math.sqrt(HEAD_DIM)
    for head in range(KV_HEADS):
        for group in range(GROUPS):
            at = (head * GROUPS + group) * HEAD_DIM
            query = turn(queries[at : at + HEAD_DIM], cosine, sine_table) * scale
            query_ref[head, :, group * rows : (group + 1) * rows] = query.astype(jnp.bfloat16)
    nothing = jnp.zeros((HEAD_DIM, rows), jnp.bfloat16)
    for head in range(KV_HEADS):
        for group in range(GROUPS):
            piece = slice(group * rows, (group + 1) * rows)
            query_pad[head, piece, :] = jnp.concatenate(
                [query_ref[head, :, piece], nothing], axis=0
            ).T
    weights[7].wait()
    turned_cotangent[...] = cotangent_ref[...].T
    acc[...] = jnp.zeros_like(acc)
    top[...] = jnp.full_like(top, MASKED)
    id_row = jnp.concatenate([id_ref[...].astype(jnp.float32)] * GROUPS, axis=1)
    local = jnp.concatenate([lax.broadcasted_iota(jnp.int32, (1, rows), 1)] * GROUPS, axis=1)
    index = place * rows + local
    ones = jnp.ones((16, rows), jnp.bfloat16)

    def attend_block(chip, half, careful):
        begin = half * rows
        first = first_ref[chip] - begin
        limit = index - chip * span - begin
        inside = first <= 0
        for head in range(KV_HEADS):
            key_at = ID_ROWS + 2 * HEAD_DIM * head
            key_t = kv[chip, half, pl.ds(key_at, HEAD_DIM), :]
            value_t = kv[chip, half, pl.ds(key_at + HEAD_DIM, HEAD_DIM), :]
            scores = transposed_times(key_t, query_ref[head])
            old = top[head]
            if careful:
                key_index = lax.broadcasted_iota(jnp.int32, scores.shape, 0)
                allowed = (key_index >= first) & (key_index <= limit)
                scores = jnp.where(allowed, scores, 2 * MASKED)
            new = jnp.maximum(old, jnp.max(scores, axis=0, keepdims=True))
            less = new
            if not careful:
                new = jnp.where(inside, new, old)
                less = jnp.where(inside, new, -MASKED)
            probs = jnp.exp2(scores - less).astype(jnp.bfloat16)
            acc[head] = acc[head] * jnp.exp2(old - new) + matmul(
                jnp.concatenate([value_t, ones], axis=0), probs
            )
            top[head] = new

    def one_block(turn_number, carry):
        chip, mates = level - lax.div(turn_number, 2), lax.rem(turn_number, 2)
        half = core + mates * (1 - 2 * core)
        block = 2 * chip + half

        @pl.when(chip >= 0)
        def _():
            for head in range(KV_HEADS):
                @pl.when((mates == 0) & (chip < level))
                def _(head=head):
                    upward(chip, head).wait_recv()
                    hand_on(chip, head)

                @pl.when(mates == 1)
                def _(head=head):
                    across(chip, head).wait_recv()

            @pl.when(mates == 1)
            def _():
                first_ref[chip] = first_allowed(kv, chip, id_row)

            @pl.when(mates == 0)
            def _():
                first_ref[chip] = first_in_half(kv, chip, core, id_row) + half * rows

            edge = (block == 0) | (block == place)

            @pl.when((block <= place) & edge)
            def _():
                attend_block(chip, half, True)

            @pl.when((block < place) & jnp.logical_not(edge))
            def _():
                attend_block(chip, half, False)

        return carry

    lax.fori_loop(0, 2 * levels, one_block, 0)
    for head in range(KV_HEADS):
        total = acc[head, HEAD_DIM : HEAD_DIM + 1, :]
        result = acc[head, :HEAD_DIM, :] * (1.0 / total)
        attended[head] = result
        top[head] = top[head] + jnp.log2(total)
        for group in range(GROUPS):
            at = (head * GROUPS + group) * HEAD_DIM
            piece = result[:, group * rows : (group + 1) * rows]
            mixed_t[pl.ds(at, HEAD_DIM), :] = piece.astype(jnp.bfloat16)

    for copy in weights[3:7]:
        copy.wait()
    residual = x_ref[...].astype(jnp.float32) + transposed_times(out_w[...], mixed_t[...])
    mean = jnp.sum(residual * residual, axis=0, keepdims=True) * (1.0 / features)
    inverse_ffn = lax.rsqrt(mean + NORM_EPS)
    ffn_gain = as_column(ffn_gain_ref[...].reshape(1, features))
    normed_ffn_t = (residual * inverse_ffn * ffn_gain).astype(jnp.bfloat16)
    normed_ffn = normed_ffn_t.T
    cotangent_t = cotangent_ref[...]
    cotangent = turned_cotangent[...]
    residual_t[...] = residual
    unit_t[...] = residual * inverse_ffn
    normed_grad[...] = jnp.zeros_like(normed_grad)
    for number, at in enumerate(range(0, wide, FF_CHUNK)):
        piece = slice(at, at + FF_CHUNK)
        gate = matmul(normed_ffn, gate_w[:, piece])
        up = matmul(normed_ffn, up_w[:, piece])
        sigmoid = 1.0 / (1.0 + jnp.exp(-gate))
        silu = gate * sigmoid
        hidden = (silu * up).astype(jnp.bfloat16)
        at_row = 2 * features * number
        stack_halves(down_part, at_row, matmul(cotangent_t, hidden))
        streams[3 * number].run(0, carries)
        grad_hidden = matmul(cotangent, down_w[:, piece])
        gate_grad = (grad_hidden * up * sigmoid * (1.0 + gate * (1.0 - sigmoid))).astype(
            jnp.bfloat16
        )
        up_grad = (grad_hidden * silu).astype(jnp.bfloat16)
        stack_halves(gate_part, at_row, matmul(normed_ffn_t, gate_grad))
        streams[3 * number + 1].run(0, carries)
        stack_halves(up_part, at_row, matmul(normed_ffn_t, up_grad))
        streams[3 * number + 2].run(0, carries)
        residual_t[...] += times_transposed(down_w[:, piece], hidden)
        normed_grad[...] += times_transposed(gate_w[:, piece], gate_grad) + times_transposed(
            up_w[:, piece], up_grad
        )
        pump(number)
    layer_out[...] = residual_t[...].astype(jnp.bfloat16)
    unit = unit_t[...]
    grad_normed = normed_grad[...]
    gain_grad = jnp.sum(grad_normed * unit, axis=1, keepdims=True)
    inner = grad_normed * ffn_gain
    mean = jnp.sum(inner * unit, axis=0, keepdims=True) * (1.0 / features)
    branch = cotangent_t.astype(jnp.float32) + inverse_ffn * (inner - unit * mean)
    residual_t[...] = branch
    branch = branch.astype(jnp.bfloat16)
    out_grads = times_transposed(mixed_t[...], branch)
    fill = jnp.broadcast_to(gain_grad, (features, out_part.shape[0] - features)).T
    lanes = out_part.shape[1]
    out_part[:features, :] = with_lanes(out_grads, lanes).astype(jnp.bfloat16)
    out_part[features:, :] = with_lanes(fill, lanes).astype(jnp.bfloat16)
    streams[3 * chunks].run(0, carries)
    mixed_grad = matmul(out_w[...], branch).astype(jnp.bfloat16)
    for head in range(KV_HEADS):
        for group in range(GROUPS):
            at = (head * GROUPS + group) * HEAD_DIM
            piece = slice(group * rows, (group + 1) * rows)
            grad = mixed_grad[at : at + HEAD_DIM, :]
            grad_ref[head, :, piece] = grad
            delta_ref[head, :, piece] = jnp.sum(
                grad.astype(jnp.float32) * attended[head, :, piece], axis=0, keepdims=True
            )
            grad_pad[head, piece, :] = jnp.concatenate([nothing, grad], axis=0).T
    pump(chunks)
    back[...] = jnp.zeros_like(back)

    def attend_back(step, half, careful):
        head = lax.div(step, levels)
        chip = lax.rem(step, levels)
        key_at = pl.multiple_of(ID_ROWS + 2 * HEAD_DIM * head, 16)
        value_at = pl.multiple_of(ID_ROWS + 2 * HEAD_DIM * head + HEAD_DIM, 16)
        begin = half * rows
        first = first_ref[chip] - begin
        limit = index - chip * span - begin
        less = top[head]
        if not careful:
            less = jnp.where(first <= 0, less, -MASKED)
        for at in range(0, rows, BACK_CHUNK):
            size = min(BACK_CHUNK, rows - at)
            key_t = kv[chip, half, pl.ds(key_at, HEAD_DIM), at : at + size]
            value_t = kv[chip, half, pl.ds(value_at, HEAD_DIM), at : at + size]
            scores = transposed_times(key_t, query_ref[head])
            if careful:
                key_index = at + lax.broadcasted_iota(jnp.int32, scores.shape, 0)
                allowed = (key_index >= first) & (key_index <= limit)
                scores = jnp.where(allowed, scores, MASKED)
            probs = jnp.exp2(scores - less)
            prob_grad = transposed_times(value_t, grad_ref[head])
            score_grad = (probs * (prob_grad - delta_ref[head])).astype(jnp.bfloat16)
            kv_back = matmul(score_grad, query_pad[head]) + matmul(
                probs.astype(jnp.bfloat16), grad_pad[head]
            )
            part[step, pl.ds(pl.multiple_of(begin + at, 128), size), :] = kv_back.astype(
                jnp.bfloat16
            )
            back[head] += matmul(key_t, score_grad)

    mate_rows = pl.ds(pl.multiple_of((1 - core) * rows, 128), rows)

    def to_mate(step):
        return pltpu.make_async_remote_copy(
            src_ref=part.at[step, mate_rows], dst_ref=from_mate.at[step],
            send_sem=mate_send.at[step], recv_sem=mate_recv.at[step],
            device_id=mate, device_id_type=MESH,
        )

    def to_below(step):
        return pltpu.make_async_remote_copy(
            src_ref=part.at[step, own], dst_ref=from_above.at[step],
            send_sem=down_send.at[step], recv_sem=above_recv.at[step],
            device_id=below, device_id_type=MESH,
        )

    def collect(step):
        chip = lax.rem(step, levels)
        to_mate(step).wait_recv()
        both = part[step, own, :].astype(jnp.float32) + from_mate[step].astype(jnp.float32)
        part[step, own, :] = both.astype(jnp.bfloat16)

        @pl.when(level < levels - 1)
        def _():
            to_below(step).wait_recv()
            more = part[step, own, :].astype(jnp.float32) + from_above[step].astype(jnp.float32)
            part[step, own, :] = more.astype(jnp.bfloat16)

        @pl.when(chip < level)
        def _():
            to_below(step).start()

    base = (place * rows).astype(jnp.float32) * inverse_in[...]
    base_cosine, base_sine = jnp.cos(base), -jnp.sin(base)
    back_cosine[...] = base_cosine * cosine_in[...] + base_sine * sine_in[...]
    back_sine[...] = base_sine * cosine_in[...] - base_cosine * sine_in[...]

    def head_done(head):
        cosine, sine_table = back_cosine[...], back_sine[...]
        step = head * levels + level
        both = part[step, own, :].astype(jnp.float32).T
        key_back = turn(both[:HEAD_DIM] * LN2, cosine, sine_table).astype(jnp.bfloat16)
        value_back = both[HEAD_DIM:].astype(jnp.bfloat16)
        kv_back = jnp.concatenate([key_back, value_back], axis=0)
        at = pl.multiple_of(head * 2 * HEAD_DIM, 2 * HEAD_DIM)
        turned_kv[pl.ds(at, 2 * HEAD_DIM), :] = kv_back
        kv_part[pl.ds(at, 2 * HEAD_DIM), :] = with_lanes(
            times_transposed(kv_back, normed_t[...]), kv_part.shape[1]
        ).astype(jnp.bfloat16)
        query_back = jnp.concatenate(
            [
                turn(
                    back[head, :, group * rows : (group + 1) * rows] * (1.0 / math.sqrt(HEAD_DIM)),
                    cosine, sine_table,
                ).astype(jnp.bfloat16)
                for group in range(GROUPS)
            ],
            axis=0,
        )
        wide_at = pl.multiple_of(head * GROUPS * HEAD_DIM, HEAD_DIM)
        turned_query[pl.ds(wide_at, GROUPS * HEAD_DIM), :] = query_back
        query_grads = with_lanes(times_transposed(normed_t[...], query_back), QUERY_COLUMNS)
        stack_halves(query_part, 2 * head * features, query_grads)

    def one_step(turn_number, carry):
        step, own_turn = lax.div(turn_number, 2), lax.rem(turn_number, 2)
        half = core + (1 - own_turn) * (1 - 2 * core)
        chip = lax.rem(step, levels)
        block = 2 * chip + half

        @pl.when((step < count) & (chip <= level))
        def _():
            edge = (block == 0) | (block == place)

            @pl.when((block <= place) & edge)
            def _():
                attend_back(step, half, True)

            @pl.when((block < place) & jnp.logical_not(edge))
            def _():
                attend_back(step, half, False)

            @pl.when(block > place)
            def _():
                part[step, mate_rows, :] = jnp.zeros((rows, 2 * HEAD_DIM), jnp.bfloat16)

            @pl.when(own_turn == 0)
            def _():
                to_mate(step).start()

        due = step - levels + level

        @pl.when((own_turn == 1) & (due >= 0) & (due < count))
        def _():
            @pl.when(lax.rem(due, levels) <= level)
            def _():
                collect(due)

        ended = lax.div(step, levels) - 1

        @pl.when((own_turn == 1) & (step > 0) & (lax.rem(step, levels) == 0))
        def _():
            head_done(ended)
            for head in range(KV_HEADS):
                @pl.when(ended == head)
                def _(head=head):
                    streams[3 * chunks + 1 + 2 * head].run(0, carries)
                    streams[3 * chunks + 2 + 2 * head].run(0, carries)

        for begin in range(0, 2 * (count + 1), SLOTS):
            some = range(begin, begin + SLOTS)

            @pl.when((turn_number >= begin) & (turn_number < begin + SLOTS))
            def _(some=some):
                for number in some:
                    if number + chunks + 1 in pumps:
                        @pl.when(turn_number == number)
                        def _(slot=number + chunks + 1):
                            pump(slot)

        return carry

    lax.fori_loop(0, 2 * (count + 1), one_step, 0)

    grad_t = matmul(query_w[...], turned_query[...])
    for head in range(KV_HEADS):
        at = head * HEAD_DIM
        weight = jnp.concatenate(
            [key_w[at : at + HEAD_DIM, :], value_w[at : at + HEAD_DIM, :]], axis=0
        )
        grad_t += transposed_times(weight, turned_kv[2 * at : 2 * at + 2 * HEAD_DIM, :])
    x = x_ref[...].astype(jnp.float32)
    mean = jnp.sum(x * x, axis=0, keepdims=True) * (1.0 / features)
    inverse_attn = lax.rsqrt(mean + NORM_EPS)
    unit = x * inverse_attn
    gain_column = jnp.sum(grad_t * unit, axis=1, keepdims=True)
    gain_rows = jnp.broadcast_to(gain_column, (features, 128)).T
    gain_part[...] = with_lanes(gain_rows[: gain_part.shape[0]], gain_part.shape[1]).astype(
        jnp.bfloat16
    )
    streams[-1].run(0, carries)
    first_ops = len(after) // 3
    for number, op in after[:first_ops]:
        streams[number].run(op, carries)
    inner = grad_t * as_column(attn_gain_ref[...].reshape(1, features))
    mean = jnp.sum(inner * unit, axis=0, keepdims=True) * (1.0 / features)
    input_grad[...] = (residual_t[...] + inverse_attn * (inner - unit * mean)).astype(jnp.bfloat16)
    for number, op in after[first_ops:]:
        streams[number].run(op, carries)
    for stream in streams:
        stream.drain(carries)

    def ended(step, carry):
        chip = lax.rem(step, levels)

        @pl.when(chip <= level)
        def _():
            to_mate(step).wait_send()

        @pl.when(chip < level)
        def _():
            to_below(step).wait_send()

        return carry

    lax.fori_loop(0, count, ended, 0)

    def handed_on(chip, carry):
        @pl.when(chip <= level)
        def _():
            for head in range(KV_HEADS):
                across(chip, head).wait_send()

                @pl.when(level < levels - 1)
                def _(head=head):
                    upward(chip, head).wait_send()

        return carry

    lax.fori_loop(0, levels, handed_on, 0)


def rotary_tables(rows):
    half_size = HEAD_DIM // 2
    inverse = (ROPE_BASE ** (-np.arange(half_size, dtype=np.float64) * 2.0 / HEAD_DIM))[:, None]
    phase = inverse * np.arange(rows, dtype=np.float64)[None, :]
    return tuple(
        jnp.asarray(table, jnp.float32) for table in (np.cos(phase), np.sin(phase), inverse)
    )


def layer(x_t, ids, attn_gain, ffn_gain, w_query, w_key_t, w_value_t, w_out, w_gate, w_up,
          w_down_t, cotangent_t):
    dp_count, ctx_count = lax.axis_size("dp"), lax.axis_size("ctx")
    order = plane_order(dp_count)
    crossed = crossed_order(order, ctx_count)
    level_bits = (ctx_count // 2).bit_length() - 1
    levels = ctx_count // 2
    features, rows = x_t.shape
    wide = w_gate.shape[1]
    span, queries = 2 * rows, GROUPS * rows
    count = KV_HEADS * levels
    chunks = wide // FF_CHUNK

    jobs = [(True, "rrr", (2 * features, FF_CHUNK // 2))] * (3 * chunks)
    jobs += [(True, "rrr", (OUT_ROWS, OUT_ROWS))]
    for head in range(KV_HEADS):
        folded = head < KV_HEADS - 1
        jobs += [
            (folded, "rrr", (2 * features, QUERY_COLUMNS // 2)),
            (folded, "rrr", (2 * HEAD_DIM, OUT_ROWS)),
        ]
    jobs += [(False, "", (16, OUT_ROWS))]
    slots = [FEED_US * number for number in range(chunks)]
    slots.append(slots[-1] + OUT_US)
    turns = 2 * (count + 1)
    slots += [slots[-1] + STEP_US * (number + 1) for number in range(turns)]
    slots.append(slots[-1] + TAIL_US)
    begins = [number // 3 for number in range(3 * chunks)] + [chunks]
    for head in range(KV_HEADS):
        begins += [chunks + 2 * (head + 1) * levels + 2] * 2
    begins += [len(slots) - 1]
    relayed = [
        chunks + 2 + 2 * step for step in range(count) if step % levels < levels - 1
    ]
    pumps, after = {}, []
    for slot, number, op in planned(
        [
            (
                len(order), 0 if folded else level_bits, level_bits, cuts, 2 * shape[0] * shape[1],
                begin,
            )
            for (folded, cuts, shape), begin in zip(jobs, begins)
        ],
        slots, relayed,
    ):
        if op == 0:
            continue
        if slot <= chunks + turns:
            pumps.setdefault(slot, []).append((number, op))
        else:
            after.append((number, op))

    vmem = lambda shape, dtype=jnp.bfloat16: pltpu.VMEM(shape, dtype)
    lands = [
        [
            vmem(size)
            for size in (
                landing_shapes(*shape, cuts, len(order), level_bits)
                if folded
                else landing_shapes(*shape, cuts, len(crossed), 0)
            )
        ]
        for folded, cuts, shape in jobs
    ]
    dma = lambda *shape: pltpu.SemaphoreType.DMA(shape)
    semaphores = len(order) + level_bits + HALVINGS + 2
    head_t = (KV_HEADS, HEAD_DIM, queries)
    padded = (KV_HEADS, queries, 2 * HEAD_DIM)
    row = (KV_HEADS, 1, queries)
    f32 = jnp.float32
    totals = [(2 * features * chunks, FF_CHUNK // 2)] * 3 + [(OUT_ROWS, OUT_ROWS)]
    totals += [(2 * KV_HEADS * features, QUERY_COLUMNS // 2), (2 * KV_HEADS * HEAD_DIM, OUT_ROWS)]
    totals += [(16, OUT_ROWS)]
    anywhere = pl.BlockSpec(memory_space=pl.ANY)
    return pl.pallas_call(
        functools.partial(layer_kernel, order, crossed, level_bits, jobs, pumps, after),
        out_shape=tuple(
            jax.ShapeDtypeStruct(shape, jnp.bfloat16) for shape in [(features, rows)] * 2 + totals
        ),
        in_specs=in_vmem(7) + [anywhere] * 8,
        out_specs=tuple(in_vmem(2) + [anywhere] * 7),
        scratch_shapes=[
            vmem(w_query.shape), vmem(w_key_t.shape), vmem(w_value_t.shape), vmem(w_out.shape),
            vmem(w_gate.shape), vmem(w_up.shape), vmem(w_down_t.shape), vmem((features, rows)),
            vmem((levels, 2, ID_ROWS + 2 * KV_HEADS * HEAD_DIM, rows)),
            vmem(head_t), vmem(padded), vmem(head_t), vmem(padded),
            vmem((levels, 1, queries), jnp.int32),
            vmem((features, rows)),
            vmem(head_t, f32),
            vmem((KV_HEADS, HEAD_DIM + 16, queries), f32),
            vmem(row, f32), vmem(row, f32),
            vmem((features, rows)),
            *[vmem((features, rows), f32) for _ in range(3)],
            vmem(head_t, f32),
            vmem((count, span, 2 * HEAD_DIM)),
            vmem((count, rows, 2 * HEAD_DIM)), vmem((count, rows, 2 * HEAD_DIM)),
            vmem((2 * KV_HEADS * HEAD_DIM, rows)), vmem((HEADS * HEAD_DIM, rows)),
            vmem((HEAD_DIM // 2, rows), f32), vmem((HEAD_DIM // 2, rows), f32),
            vmem((rows, features)),
            *[vmem(shape) for shape in totals],
            lands,
            dma(8),
            *[dma(levels, KV_HEADS) for _ in range(4)],
            *[dma(count) for _ in range(4)],
            dma(len(jobs), semaphores), dma(len(jobs), semaphores),
        ],
        compiler_params=pltpu.CompilerParams(
            collective_id=1, has_side_effects=True, vmem_limit_bytes=60 * 1024 * 1024
        ),
        name="layer",
    )(
        x_t, ids, attn_gain, ffn_gain, *rotary_tables(rows), w_query, w_key_t, w_value_t, w_out,
        w_gate, w_up, w_down_t, cotangent_t,
    )


PIECES = 2
SOME_ROWS = 48


def finish_kernel(
    layer_in, input_in, gate, up, down_t, out, query, kv, gain,
    layer_out, input_out, gate_out, up_out, down_out, out_out, key_out, value_out, query_out,
    gain_ffn, gain_attn,
    held, made, out_held, out_made, query_held, query_made, kv_held, key_made, value_made, passed,
    come, go,
):
    features, wide_columns = gate_out.shape
    piece = features // PIECES
    stacked = wide_columns // gate.shape[1]
    passed_in = [
        pltpu.make_async_copy(source, passed.at[number], come.at[3 * PIECES + 3 + number])
        for number, source in enumerate((layer_in, input_in))
    ]
    passed_out = [
        pltpu.make_async_copy(passed.at[number], target, go.at[number])
        for number, target in enumerate((layer_out, input_out))
    ]
    wide = []
    for number, (source, target) in enumerate(
        ((gate, gate_out), (up, up_out), (down_t, down_out))
    ):
        arrival = pltpu.make_async_copy(source, held.at[number], come.at[number])
        departures = []
        for at in range(PIECES):
            rows = pl.ds(at * piece, piece)
            departures.append(
                pltpu.make_async_copy(
                    made.at[number, rows], target.at[rows], go.at[2 + number * PIECES + at]
                )
            )
        wide.append((arrival, departures))
    at = 3 * PIECES
    small_in = [
        pltpu.make_async_copy(source, target, come.at[at + number])
        for number, (source, target) in enumerate(
            ((out, out_held), (query, query_held), (kv, kv_held))
        )
    ]
    small_out = [
        pltpu.make_async_copy(source, target, go.at[2 + at + number])
        for number, (source, target) in enumerate(
            (
                (out_made, out_out), (query_made, query_out), (key_made, key_out),
                (value_made, value_out),
            )
        )
    ]
    for arrival, _ in wide:
        arrival.start()
    for copy in small_in + passed_in:
        copy.start()

    def by_rows(count, convert):
        def some(step, carry):
            convert(pl.ds(pl.multiple_of(step * SOME_ROWS, 16), SOME_ROWS), step * SOME_ROWS)
            return carry

        lax.fori_loop(0, count // SOME_ROWS, some, 0)

    for number, (arrival, departures) in enumerate(wide):
        arrival.wait()
        for at in range(PIECES):

            def convert(rows, start, number=number, skip=at * piece):
                made[
                    number, pl.ds(pl.multiple_of(skip + start, 16), SOME_ROWS), :
                ] = jnp.concatenate(
                    [
                        held[
                            number,
                            pl.ds(pl.multiple_of(column * features + skip + start, 16), SOME_ROWS),
                            :,
                        ].astype(jnp.float32)
                        for column in range(stacked)
                    ],
                    axis=1,
                )

            by_rows(piece, convert)
            departures[at].start()

    small_in[0].wait()

    def convert_out(rows, start):
        out_made[rows, :] = out_held[rows, :].astype(jnp.float32)[:, :features]

    by_rows(features, convert_out)
    small_out[0].start()
    gain_ffn[...] = out_held[OUT_ROWS - 16 :, :].astype(jnp.float32)[-1:, :features].reshape(features)
    small_in[1].wait()
    width = GROUPS * HEAD_DIM

    def convert_query(rows, start):
        pieces = []
        for number in range(2 * KV_HEADS):
            at = pl.multiple_of(number * features + start, 16)
            values = query_held[pl.ds(at, SOME_ROWS), :].astype(jnp.float32)
            pieces.append(values[:, : width - values.shape[1]] if number % 2 else values)
        query_made[rows, :] = jnp.concatenate(pieces, axis=1)

    by_rows(features, convert_query)
    small_out[1].start()
    gain_attn[...] = gain[...].astype(jnp.float32)[-1:, :features].reshape(features)
    small_in[2].wait()
    for head in range(KV_HEADS):
        at = head * HEAD_DIM
        both = kv_held[2 * at : 2 * at + 2 * HEAD_DIM, :].astype(jnp.float32)[:, :features]
        key_made[at : at + HEAD_DIM, :] = both[:HEAD_DIM]
        value_made[at : at + HEAD_DIM, :] = both[HEAD_DIM:]
    small_out[2].start()
    small_out[3].start()
    for arrival, departure in zip(passed_in, passed_out):
        arrival.wait()
        departure.start()
    for copy in passed_out + [copy for _, copies in wide for copy in copies] + small_out:
        copy.wait()


def finish(layer_t, input_t, down_t, gate, up, out, query, kv, gain):
    features = layer_t.shape[0]
    wide = gate.shape[0] * gate.shape[1] // features
    key_width = KV_HEADS * HEAD_DIM
    f32 = jnp.float32
    anywhere = pl.BlockSpec(memory_space=pl.ANY)
    shape = lambda *dims: jax.ShapeDtypeStruct(dims, f32)
    short = jax.ShapeDtypeStruct(layer_t.shape, layer_t.dtype)
    vmem = lambda *dims: pltpu.VMEM(dims, jnp.bfloat16)
    vmem_f32 = lambda *dims: pltpu.VMEM(dims, f32)
    copies = 3 * PIECES
    return pl.pallas_call(
        finish_kernel,
        out_shape=(
            short, short,
            shape(features, wide), shape(features, wide), shape(features, wide),
            shape(features, features), shape(key_width, features), shape(key_width, features),
            shape(features, features), shape(features), shape(features),
        ),
        in_specs=[anywhere] * 8 + in_vmem(1),
        out_specs=tuple([anywhere] * 9 + in_vmem(2)),
        scratch_shapes=[
            vmem(3, *gate.shape), vmem_f32(3, features, wide),
            vmem(*out.shape), vmem_f32(features, features),
            vmem(*query.shape), vmem_f32(features, features),
            vmem(*kv.shape), vmem_f32(key_width, features), vmem_f32(key_width, features),
            vmem(2, *layer_t.shape),
            pltpu.SemaphoreType.DMA((copies + 5,)), pltpu.SemaphoreType.DMA((copies + 6,)),
        ],
        compiler_params=pltpu.CompilerParams(vmem_limit_bytes=60 * 1024 * 1024),
        name="finish",
    )(layer_t, input_t, gate, up, down_t, out, query, kv, gain)


def in_vmem(count):
    return [pl.BlockSpec(memory_space=pltpu.VMEM)] * count


def on_device(
    hidden_in, segment_ids, w_query, w_key, w_value, w_out, w_gate, w_up, w_down, gain_attn,
    gain_ffn, out_grad,
):
    summed = layer(
        hidden_in[0].T, segment_ids, gain_attn, gain_ffn, w_query, w_key.T, w_value.T,
        w_out, w_gate, w_up, w_down.T, out_grad[0].T,
    )
    (
        layer_t, input_t, grad_gate, grad_up, grad_down_t, grad_out, grad_key_t, grad_value_t,
        grad_query, grad_gain_ffn, grad_gain_attn,
    ) = finish(*summed)
    return (
        layer_t.T[None], input_t.T[None], grad_query, grad_key_t.T, grad_value_t.T, grad_out,
        grad_gate, grad_up, grad_down_t.T, grad_gain_attn, grad_gain_ffn,
    )


def solution(mesh):
    rows = P("dp", "ctx", None)
    return jax.shard_map(
        on_device,
        mesh=mesh,
        in_specs=(rows, P("dp", "ctx")) + (P(),) * 9 + (rows,),
        out_specs=(rows, rows) + (P(),) * 9,
        check_vma=False,
    )
```
